32 devices in a mesh: groups: 2 (over y), frame: 4 (over z), quarter: 2 (over x), sub: 2 (over core).
Axes of the slice: x: 2, y: 2, z: 4, core: 2. Of those that a mesh axis runs over, the one named last changes fastest.
Arguments:
- queries: bfloat16 [16, 1024, 256], P(('groups', 'frame'), ('quarter', 'sub')), parts along dimension 0, may hold values from -36 to 36
- keys: bfloat16 [16, 1024, 256], P(('groups', 'frame'), ('quarter', 'sub')), parts along dimension 0, may hold values from -6 to 6
- values: bfloat16 [16, 1024, 256], P(('groups', 'frame'), ('quarter', 'sub')), parts along dimension 0, may hold values from -6 to 6
Outputs:
- attended: bfloat16 [16, 1024, 256], P(('groups', 'frame'), ('quarter', 'sub')), parts along dimension 0
The draws below stay inside these ranges and needn't reach their ends.
There are 2 independent parts, one for each index of `groups`. The reference program is written for one: setup_inputs(seed, part) draws one part's arguments, and reference() takes and returns one part's arrays. A program takes and returns all parts, laid end to end along the dimension named above; each array names one. Nothing has to cross between parts.
All inputs are finite; a program needn't handle non-finite values.
Results may differ from the reference program's by a relative error of at most 0.0028.
Values may be sent and summed in bfloat16 or wider, within the bound.
No kernel may reach another device: no remote copies, remote signals or barrier semaphores. Data moves between devices by JAX's collectives and lax.ppermute only.
A program may use at most 64 MiB of HBM per device.

```python
import math
import jax
import jax.numpy as jnp
from jax import lax

HEAD_DIM = 128
STRIP = 16
FRAMES = 8
POS = 1024


def draw_keys(key, part):
    shape = (FRAMES, POS, 2 * HEAD_DIM)
    result = jnp.clip(jax.random.normal(jax.random.fold_in(key, 1), shape, jnp.float32), -6.0, 6.0)
    return result.astype(jnp.bfloat16)


def draw_queries(key, part):
    shape = (FRAMES, POS, 2 * HEAD_DIM)
    result = jnp.clip(3.0 * jax.random.normal(jax.random.fold_in(key, 201), shape, jnp.float32), -18.0, 18.0)
    return result.astype(jnp.bfloat16)


def block_scale(stream_key, shape, split, smallest, high):
    def one(axis_at, shards_of):
        steps = jax.random.uniform(jax.random.fold_in(jax.random.fold_in(stream_key, 6), axis_at), (shards_of,), jnp.float32, smallest / len(split), high / len(split))
        return jnp.repeat(jnp.exp(steps), shape[axis_at] // shards_of).reshape((-1,) + (1,) * (len(shape) - axis_at - 1))

    loudness = one(*split[0])
    for cut in split[1:]:
        loudness = loudness * one(*cut)
    return loudness


def normal_values(stream_key, extent, spread, reach, cuts=(), dtype=jnp.bfloat16):
    values = jax.random.normal(stream_key, extent, jnp.float32) * spread
    if len(cuts) > 0:
        values = block_scale(stream_key, extent, cuts, -0.22, 0.18) * values
    return jnp.clip(values, min=-reach, max=reach).astype(dtype)


def setup_inputs(seed: int = 0, part: int = 0) -> dict:
    seeds = jax.random.split(jax.random.key(seed), 4)
    part_keys = jax.random.split(jax.random.fold_in(seeds[3], part), 4)
    queries = draw_queries(jax.random.fold_in(jax.random.fold_in(seeds[3], part), 71), part)
    keys = draw_keys(jax.random.fold_in(jax.random.fold_in(seeds[3], part), 71), part)
    values = normal_values(part_keys[2], (FRAMES, POS, 2 * HEAD_DIM), 1.0, 6.0, ((0, 4), (1, 4)))
    return {"queries": queries, "keys": keys, "values": values}


def attend(query_rows, key_rows, value_rows):
    width = query_rows.shape[-1]
    scores = jnp.dot(query_rows, key_rows.T, preferred_element_type=jnp.float32) * (1.0 / math.sqrt(width))
    highest = lax.optimization_barrier(jnp.max(scores, axis=-1, keepdims=True))
    expo = jnp.exp(scores - highest)
    totals = lax.optimization_barrier(jnp.sum(expo, axis=-1, keepdims=True))
    mixed = jnp.dot(expo.astype(jnp.bfloat16), value_rows, preferred_element_type=jnp.float32)
    return (mixed / totals).astype(jnp.bfloat16)

def reference(queries, keys, values):
    block_rows = math.gcd(POS, 1024)
    block_count = POS // block_rows

    def spatial_frame(frame_data):
        query_frame, key_frame, value_frame = frame_data
        grouped = query_frame.reshape(block_count, block_rows, HEAD_DIM)
        mixed = lax.map(lambda block: attend(block, key_frame, value_frame), grouped)
        return mixed.reshape(POS, HEAD_DIM)
    spatial = lax.map(spatial_frame, (queries[..., :HEAD_DIM], keys[..., :HEAD_DIM], values[..., :HEAD_DIM]))
    strips_total = POS // STRIP

    def to_strips(array):
        part_two = array[..., HEAD_DIM:].reshape(FRAMES, strips_total, STRIP, HEAD_DIM)
        return part_two.transpose(1, 0, 2, 3).reshape(strips_total, FRAMES * STRIP, HEAD_DIM)

    def strip_attend(strip_data):
        return attend(strip_data[0], strip_data[1], strip_data[2])
    temporal = lax.map(strip_attend, (to_strips(queries), to_strips(keys), to_strips(values)))
    temporal = temporal.reshape(strips_total, FRAMES, STRIP, HEAD_DIM).transpose(1, 0, 2, 3).reshape(FRAMES, POS, HEAD_DIM)
    return jnp.concatenate([spatial, temporal], axis=-1)
```

```python
import functools
import math

import jax
import jax.numpy as jnp
from jax import lax
from jax.experimental import pallas as pl
from jax.experimental.pallas import tpu as pltpu
from jax.sharding import PartitionSpec as P

STRIP = 16
VMEM_LIMIT = 16 * 1024 * 1024


def partner_of(index, step, count):
    if count & (count - 1) == 0:
        return index ^ step
    return (index + step) % count


def prep_kernel(count, head_width, q_hbm, k_hbm, v_hbm, *refs):
    blocks, kv_ref, sems = refs[:count], refs[count], refs[count + 1]
    me = lax.axis_index("frame")
    rows = blocks[0].shape[2]
    copies = []
    for step in [*range(count - 1, 0, -1), 0]:
        start = pl.multiple_of(partner_of(me, step, count) * rows, rows)
        for which, array in enumerate((q_hbm, k_hbm, v_hbm)):
            copies.append((array.at[:, pl.ds(start, rows), head_width:], blocks[step].at[which]))
    for which, array in enumerate((k_hbm, v_hbm)):
        copies.append((array.at[:, :, :head_width], kv_ref.at[which]))
    started = [
        pltpu.make_async_copy(src, dst, sems.at[number]) for number, (src, dst) in enumerate(copies)
    ]
    for copy in started:
        copy.start()
    for copy in started:
        copy.wait()


def attend(query_rows, key_rows, value_rows, score_scale):
    scores = (
        lax.dot_general(
            query_rows, key_rows, (((1,), (1,)), ((), ())), preferred_element_type=jnp.float32
        )
        * score_scale
    )
    highest = jnp.max(scores, axis=-1, keepdims=True)
    expo = jnp.exp(scores - highest)
    totals = jnp.sum(expo, axis=-1, keepdims=True)
    mixed = jnp.dot(expo.astype(jnp.bfloat16), value_rows, preferred_element_type=jnp.float32)
    return (mixed / totals).astype(jnp.bfloat16)


def temporal_kernel(count, score_scale, *refs):
    ins, outs = refs[:count], refs[count:]
    frames_dev, rows = ins[0].shape[1:3]
    for strip in range(rows // STRIP):
        cut = slice(strip * STRIP, (strip + 1) * STRIP)
        query, key, value = (
            jnp.concatenate([ref[which, frame, cut] for ref in ins for frame in range(frames_dev)])
            for which in range(3)
        )
        out = attend(query, key, value, score_scale)
        for number, ref in enumerate(outs):
            for frame in range(frames_dev):
                lower = (number * frames_dev + frame) * STRIP
                ref[frame, cut] = out[lower : lower + STRIP]


def spatial_kernel(score_scale, pieces, q_hbm, *refs):
    kvs, out_hbm = refs[:pieces], refs[pieces]
    q_ref, o_ref, sems = refs[pieces + 1 :]
    head_width = q_ref.shape[-1]
    load = pltpu.make_async_copy(q_hbm.at[:, :, :head_width], q_ref, sems.at[0])
    load.start()
    load.wait()
    for frame in range(q_ref.shape[0]):
        key = jnp.concatenate([kv[0, frame] for kv in kvs])
        value = jnp.concatenate([kv[1, frame] for kv in kvs])
        o_ref[frame] = attend(q_ref[frame], key, value, score_scale)
    store = pltpu.make_async_copy(o_ref, out_hbm.at[:, :, :head_width], sems.at[1])
    store.start()
    store.wait()


def join_kernel(count, head_width, *refs):
    pieces, out_hbm, sems = refs[:count], refs[count + 1], refs[count + 2]
    me = lax.axis_index("frame")
    rows = pieces[0].shape[1]
    copies = []
    for step in range(count):
        start = pl.multiple_of(partner_of(me, step, count) * rows, rows)
        copies.append(
            pltpu.make_async_copy(
                pieces[step], out_hbm.at[:, pl.ds(start, rows), head_width:], sems.at[step]
            )
        )
    for copy in copies:
        copy.start()
    for copy in copies:
        copy.wait()


def body(queries, keys, values):
    frames_dev, tokens_dev, width = queries.shape
    head_width = width // 2
    score_scale = 1.0 / math.sqrt(head_width)
    count = lax.axis_size("frame")
    rows = tokens_dev // count
    dtype = queries.dtype
    hbm = pl.BlockSpec(memory_space=pl.ANY)
    vmem = pl.BlockSpec(memory_space=pltpu.VMEM)
    params = pltpu.CompilerParams(vmem_limit_bytes=VMEM_LIMIT)

    *blocks, kv_own = pl.pallas_call(
        functools.partial(prep_kernel, count, head_width),
        out_shape=[jax.ShapeDtypeStruct((3, frames_dev, rows, head_width), dtype)] * count
        + [jax.ShapeDtypeStruct((2, frames_dev, tokens_dev, head_width), dtype)],
        in_specs=[hbm] * 3,
        out_specs=[vmem] * (count + 1),
        scratch_shapes=[pltpu.SemaphoreType.DMA((3 * count + 2,))],
        compiler_params=params,
        name="prep",
    )(queries, keys, values)

    def frame_shift(array, step, back=False):
        pairs = [(i, partner_of(i, step, count)) for i in range(count)]
        if back:
            pairs = [(b, a) for a, b in pairs]
        return lax.ppermute(array, "frame", pairs)

    arrived = [blocks[0]] + [None] * (count - 1)
    for step in range(count - 1, 0, -1):
        arrived[step] = frame_shift(blocks[step], step)

    pieces = [kv_own]
    quarters, subs = lax.axis_size("quarter"), lax.axis_size("sub")
    for step in range(1, quarters):
        pairs = [(i, (i + step) % quarters) for i in range(quarters)]
        pieces.append(lax.ppermute(kv_own, "quarter", pairs))
    for piece in list(pieces):
        for step in range(1, subs):
            pairs = [(i, (i + step) % subs) for i in range(subs)]
            pieces.append(lax.ppermute(piece, "sub", pairs))

    out = pl.pallas_call(
        functools.partial(spatial_kernel, score_scale, len(pieces)),
        out_shape=jax.ShapeDtypeStruct(queries.shape, dtype),
        in_specs=[hbm] + [vmem] * len(pieces),
        out_specs=hbm,
        scratch_shapes=[
            pltpu.VMEM((frames_dev, tokens_dev, head_width), dtype),
            pltpu.VMEM((frames_dev, tokens_dev, head_width), dtype),
            pltpu.SemaphoreType.DMA((2,)),
        ],
        compiler_params=params,
        name="spatial",
    )(queries, *pieces)

    strip_out = pl.pallas_call(
        functools.partial(temporal_kernel, count, score_scale),
        out_shape=[jax.ShapeDtypeStruct((frames_dev, rows, head_width), dtype)] * count,
        in_specs=[vmem] * count,
        out_specs=[vmem] * count,
        compiler_params=params,
        name="temporal",
    )(*arrived)

    returned = [strip_out[0]] + [None] * (count - 1)
    for step in range(count - 1, 0, -1):
        returned[step] = frame_shift(strip_out[step], step, back=True)

    return pl.pallas_call(
        functools.partial(join_kernel, count, head_width),
        out_shape=jax.ShapeDtypeStruct(queries.shape, dtype),
        in_specs=[vmem] * count + [hbm],
        out_specs=hbm,
        scratch_shapes=[pltpu.SemaphoreType.DMA((count,))],
        input_output_aliases={count: 0},
        compiler_params=params,
        name="join",
    )(*returned, out)


def solution(mesh):
    spec = P(("groups", "frame"), ("quarter", "sub"), None)
    return jax.shard_map(
        body, mesh=mesh, in_specs=(spec,) * 3, out_specs=spec, check_vma=False
    )
```

```python
import functools
import math

import jax
import jax.numpy as jnp
from jax import lax
from jax.experimental import pallas as pl
from jax.experimental.pallas import tpu as pltpu
from jax.sharding import PartitionSpec as P

STRIP = 16
VMEM_LIMIT = 16 * 1024 * 1024


def partner_of(index, step, count):
    if count & (count - 1) == 0:
        return index ^ step
    return (index + step) % count


def run_copies(copies, sems):
    started = [pltpu.make_async_copy(src, dst, sems.at[n]) for n, (src, dst) in enumerate(copies)]
    for copy in started:
        copy.start()
    for copy in started:
        copy.wait()


def prep_kernel(team, head_width, q_hbm, k_hbm, v_hbm, *refs):
    pairs, triples, refs = refs[:team], refs[team : 2 * team - 1], refs[2 * team - 1 :]
    q_own, kv_ref, q_spatial, sems = refs
    member = lax.axis_index("frame") % team
    rows = q_own.shape[1]
    starts = [pl.multiple_of((member + step) % team * rows, rows) for step in range(team)]

    def cut(array, step):
        return array.at[:, pl.ds(starts[step], rows), head_width:]

    copies = []
    for step in range(team):
        copies += [(cut(k_hbm, step), pairs[step].at[0]), (cut(v_hbm, step), pairs[step].at[1])]
    for step in range(1, team):
        copies += [
            (cut(array, step), triples[step - 1].at[which])
            for which, array in enumerate((k_hbm, v_hbm, q_hbm))
        ]
    copies.append((cut(q_hbm, 0), q_own))
    for which, array in enumerate((k_hbm, v_hbm)):
        copies.append((array.at[:, :, :head_width], kv_ref.at[which]))
    copies.append((q_hbm.at[:, :, :head_width], q_spatial))
    run_copies(copies, sems)


def score(query_rows, key_rows, score_scale):
    product = lax.dot_general(
        query_rows, key_rows, (((1,), (1,)), ((), ())), preferred_element_type=jnp.float32
    )
    return product * score_scale


def mix(expo, value_rows):
    return jnp.dot(expo.astype(jnp.bfloat16), value_rows, preferred_element_type=jnp.float32)


def temporal_kernel(team, count, passed, score_scale, *refs):
    own, own_query, mates, others = refs[0], refs[1], refs[2 : 1 + team], refs[1 + team : 1 + count]
    outs = refs[1 + count + passed : 1 + count + passed + team]
    frames_dev, rows = own_query.shape[:2]
    cuts = [slice(lower, lower + STRIP) for lower in range(0, rows, STRIP)]

    def gather(parts, cut):
        return jnp.concatenate([part[f, cut] for part in parts for f in range(frames_dev)])

    blocks = [own, *mates, *others]
    queries = [gather([own_query, *(m.at[2] for m in mates)], cut) for cut in cuts]
    keys = [gather([b.at[0] for b in blocks], cut) for cut in cuts]
    values = [gather([b.at[1] for b in blocks], cut) for cut in cuts]
    scores = [score(q, k, score_scale) for q, k in zip(queries, keys)]
    highest = [jnp.max(s, axis=-1, keepdims=True) for s in scores]
    expo = [jnp.exp(s - h) for s, h in zip(scores, highest)]
    totals = [jnp.sum(e, axis=-1, keepdims=True) for e in expo]
    mixed = [mix(e, v) for e, v in zip(expo, values)]
    results = [(m / t).astype(jnp.bfloat16) for m, t in zip(mixed, totals)]
    for cut, result in zip(cuts, results):
        for number, ref in enumerate(outs):
            for frame in range(frames_dev):
                lower = (number * frames_dev + frame) * STRIP
                ref[frame, cut] = result[lower : lower + STRIP]


def first_kernel(score_scale, pieces, q_ref, *refs):
    kvs, (top_ref, total_ref, acc_ref) = refs[:pieces], refs[pieces:]
    for frame in range(q_ref.shape[0]):
        key = jnp.concatenate([kv[0, frame] for kv in kvs])
        value = jnp.concatenate([kv[1, frame] for kv in kvs])
        scores = score(q_ref[frame], key, score_scale)
        highest = jnp.max(scores, axis=-1, keepdims=True)
        expo = jnp.exp(scores - highest)
        top_ref[frame] = highest
        total_ref[frame] = jnp.sum(expo, axis=-1, keepdims=True)
        acc_ref[frame] = mix(expo, value)


def last_kernel(score_scale, pieces, q_ref, *refs):
    kvs, (top_ref, total_ref, acc_ref, out_hbm, o_ref, sems) = refs[:pieces], refs[pieces:]
    head_width = q_ref.shape[-1]
    for frame in range(q_ref.shape[0]):
        key = jnp.concatenate([kv[0, frame] for kv in kvs])
        value = jnp.concatenate([kv[1, frame] for kv in kvs])
        scores = score(q_ref[frame], key, score_scale)
        highest = jnp.maximum(top_ref[frame], jnp.max(scores, axis=-1, keepdims=True))
        expo = jnp.exp(scores - highest)
        factor = jnp.exp(top_ref[frame] - highest)
        total = total_ref[frame] * factor + jnp.sum(expo, axis=-1, keepdims=True)
        o_ref[frame] = ((acc_ref[frame] * factor + mix(expo, value)) / total).astype(jnp.bfloat16)
    run_copies([(o_ref, out_hbm.at[:, :, :head_width])], sems)


def join_kernel(team, head_width, *refs):
    pieces, out_hbm, sems = refs[:team], refs[team + 1], refs[team + 2]
    member = lax.axis_index("frame") % team
    rows = pieces[0].shape[1]
    copies = []
    for step, piece in enumerate(pieces):
        start = pl.multiple_of((member + step) % team * rows, rows)
        copies.append((piece, out_hbm.at[:, pl.ds(start, rows), head_width:]))
    run_copies(copies, sems)


def body(queries, keys, values):
    frames_dev, tokens_dev, width = queries.shape
    head_width = width // 2
    score_scale = 1.0 / math.sqrt(head_width)
    count = lax.axis_size("frame")
    team = 2 if count & (count - 1) == 0 and count > 1 else 1
    rows = tokens_dev // team
    dtype = queries.dtype
    hbm = pl.BlockSpec(memory_space=pltpu.HBM)
    vmem = pl.BlockSpec(memory_space=pltpu.VMEM)
    anywhere = pl.BlockSpec(memory_space=pl.ANY)

    def call(kernel, name, **rest):
        return pl.pallas_call(
            kernel,
            name=name,
            compiler_params=pltpu.CompilerParams(vmem_limit_bytes=VMEM_LIMIT),
            cost_estimate=pl.CostEstimate(flops=1, bytes_accessed=1, transcendentals=0),
            **rest,
        )

    def in_vmem(*shape, of=dtype):
        return pltpu.VMEM(shape, of)

    pair, triple = ((size, frames_dev, rows, head_width) for size in (2, 3))
    whole = (frames_dev, tokens_dev, head_width)
    cut = call(
        functools.partial(prep_kernel, team, head_width),
        "prep",
        out_shape=[in_vmem(*pair)] * team
        + [in_vmem(*triple)] * (team - 1)
        + [in_vmem(*pair[1:]), in_vmem(2, *whole), in_vmem(*whole)],
        in_specs=[hbm] * 3,
        out_specs=[vmem] * (2 * team + 2),
        scratch_shapes=[pltpu.SemaphoreType.DMA((5 * team + 1,))],
    )(*(pltpu.with_memory_space_constraint(array, pltpu.HBM) for array in (queries, keys, values)))
    pairs, triples, (query_own, kv_own, query_spatial) = cut[:team], cut[team:-3], cut[-3:]

    def exchange(array, axis, step):
        size = lax.axis_size(axis)
        return lax.ppermute(array, axis, [(i, partner_of(i, step, size)) for i in range(size)])

    subs, quarters = lax.axis_size("sub"), lax.axis_size("quarter")
    others = [exchange(pairs[step % team], "frame", step) for step in range(team, count)]
    across = [exchange(kv_own, "quarter", step) for step in range(1, quarters)]
    near = [exchange(kv_own, "sub", step) for step in range(1, subs)]
    mates = [exchange(triples[step - 1], "frame", step) for step in range(1, team)]

    early = [kv_own, *near]
    state = [in_vmem(*whole[:2], size, of=jnp.float32) for size in (1, 1, head_width)]
    running = call(
        functools.partial(first_kernel, score_scale, len(early)),
        "first",
        out_shape=state,
        in_specs=[vmem] * (1 + len(early)),
        out_specs=[vmem] * 3,
    )(query_spatial, *early)

    passed = len(across)
    *strip_out, = call(
        functools.partial(temporal_kernel, team, count, passed, score_scale),
        "temporal",
        out_shape=[in_vmem(*pair[1:])] * team + [in_vmem(*kv_own.shape)] * passed,
        in_specs=[vmem] * (1 + count) + [anywhere] * passed,
        out_specs=[vmem] * team + [anywhere] * passed,
        input_output_aliases={1 + count + n: team + n for n in range(passed)},
    )(pairs[0], query_own, *mates, *others, *across)
    strip_out, across = strip_out[:team], strip_out[team:]
    far = [exchange(piece, "sub", step) for piece in across for step in range(1, subs)]
    returned = strip_out[:1] + [exchange(strip_out[step], "frame", step) for step in range(1, team)]

    late = [*across, *far]
    out = call(
        functools.partial(last_kernel, score_scale, len(late)),
        "last",
        out_shape=jax.ShapeDtypeStruct(queries.shape, dtype),
        in_specs=[vmem] * (4 + len(late)),
        out_specs=hbm,
        scratch_shapes=[pltpu.VMEM(whole, dtype), pltpu.SemaphoreType.DMA((1,))],
    )(query_spatial, *late, *running)

    return call(
        functools.partial(join_kernel, team, head_width),
        "join",
        out_shape=jax.ShapeDtypeStruct(queries.shape, dtype),
        in_specs=[vmem] * team + [hbm],
        out_specs=hbm,
        scratch_shapes=[pltpu.SemaphoreType.DMA((team,))],
        input_output_aliases={team: 0},
    )(*returned, out)


def solution(mesh):
    spec = P(("groups", "frame"), ("quarter", "sub"), None)
    return jax.shard_map(
        body, mesh=mesh, in_specs=(spec,) * 3, out_specs=spec, check_vma=False
    )
```

```python
import functools
import math

import jax
import jax.numpy as jnp
from jax import lax
from jax.experimental import pallas as pl
from jax.experimental.pallas import tpu as pltpu
from jax.sharding import PartitionSpec as P

STRIP = 16
VMEM_LIMIT = 16 * 1024 * 1024


def partner_of(index, step, count):
    if count & (count - 1) == 0:
        return index ^ step
    return (index + step) % count


def run_copies(copies, sems):
    started = [pltpu.make_async_copy(src, dst, sems.at[n]) for n, (src, dst) in enumerate(copies)]
    for copy in started:
        copy.start()
    for copy in started:
        copy.wait()


def prep_kernel(team, head_width, q_hbm, k_hbm, v_hbm, *refs):
    pairs, triples, refs = refs[:team], refs[team : 2 * team - 1], refs[2 * team - 1 :]
    q_own, kv_ref, q_spatial, sems = refs
    member = lax.axis_index("frame") % team
    rows = q_own.shape[1]
    starts = [pl.multiple_of((member + step) % team * rows, rows) for step in range(team)]

    def cut(array, step):
        return array.at[:, pl.ds(starts[step], rows), head_width:]

    copies = []
    for step in range(team):
        copies += [(cut(k_hbm, step), pairs[step].at[0]), (cut(v_hbm, step), pairs[step].at[1])]
    for step in range(1, team):
        copies += [
            (cut(array, step), triples[step - 1].at[which])
            for which, array in enumerate((k_hbm, v_hbm, q_hbm))
        ]
    copies.append((cut(q_hbm, 0), q_own))
    for which, array in enumerate((k_hbm, v_hbm)):
        copies.append((array.at[:, :, :head_width], kv_ref.at[which]))
    copies.append((q_hbm.at[:, :, :head_width], q_spatial))
    run_copies(copies, sems)


def score(query_rows, key_rows, score_scale):
    product = lax.dot_general(
        query_rows, key_rows, (((1,), (1,)), ((), ())), preferred_element_type=jnp.float32
    )
    return product * score_scale


def mix(expo, value_rows):
    return jnp.dot(expo.astype(jnp.bfloat16), value_rows, preferred_element_type=jnp.float32)


def temporal_kernel(team, count, passed, score_scale, *refs):
    own, own_query, mates, others = refs[0], refs[1], refs[2 : 1 + team], refs[1 + team : 1 + count]
    outs = refs[1 + count + passed :][:team]
    frames_dev, rows = own_query.shape[:2]
    cuts = [slice(lower, lower + STRIP) for lower in range(0, rows, STRIP)]

    def gather(parts, cut):
        return jnp.concatenate([part[f, cut] for part in parts for f in range(frames_dev)])

    blocks = [own, *mates, *others]
    queries = [gather([own_query, *(m.at[2] for m in mates)], cut) for cut in cuts]
    keys = [gather([b.at[0] for b in blocks], cut) for cut in cuts]
    values = [gather([b.at[1] for b in blocks], cut) for cut in cuts]
    scores = [score(q, k, score_scale) for q, k in zip(queries, keys)]
    highest = [jnp.max(s, axis=-1, keepdims=True) for s in scores]
    expo = [jnp.exp(s - h) for s, h in zip(scores, highest)]
    totals = [jnp.sum(e, axis=-1, keepdims=True) for e in expo]
    mixed = [mix(e, v) for e, v in zip(expo, values)]
    results = [(m / t).astype(jnp.bfloat16) for m, t in zip(mixed, totals)]
    for cut, result in zip(cuts, results):
        for number, ref in enumerate(outs):
            for frame in range(frames_dev):
                lower = (number * frames_dev + frame) * STRIP
                ref[frame, cut] = result[lower : lower + STRIP]


def first_kernel(score_scale, pieces, q_ref, *refs):
    kvs, (top_ref, total_ref, acc_ref) = refs[:pieces], refs[pieces:]
    for frame in range(q_ref.shape[0]):
        key = jnp.concatenate([kv[0, frame] for kv in kvs])
        value = jnp.concatenate([kv[1, frame] for kv in kvs])
        scores = score(q_ref[frame], key, score_scale)
        highest = jnp.max(scores, axis=-1, keepdims=True)
        expo = jnp.exp(scores - highest)
        top_ref[frame] = highest
        total_ref[frame] = jnp.sum(expo, axis=-1, keepdims=True)
        acc_ref[frame] = mix(expo, value)


def last_kernel(score_scale, pieces, q_ref, *refs):
    kvs, (top_ref, total_ref, acc_ref, out_hbm, o_ref, sems) = refs[:pieces], refs[pieces:]
    head_width = q_ref.shape[-1]
    for frame in range(q_ref.shape[0]):
        key = jnp.concatenate([kv[0, frame] for kv in kvs])
        value = jnp.concatenate([kv[1, frame] for kv in kvs])
        scores = score(q_ref[frame], key, score_scale)
        highest = jnp.maximum(top_ref[frame], jnp.max(scores, axis=-1, keepdims=True))
        expo = jnp.exp(scores - highest)
        factor = jnp.exp(top_ref[frame] - highest)
        total = total_ref[frame] * factor + jnp.sum(expo, axis=-1, keepdims=True)
        o_ref[frame] = ((acc_ref[frame] * factor + mix(expo, value)) / total).astype(jnp.bfloat16)
    run_copies([(o_ref, out_hbm.at[:, :, :head_width])], sems)


def join_kernel(team, head_width, *refs):
    pieces, out_hbm, sems = refs[:team], refs[team + 1], refs[team + 2]
    member = lax.axis_index("frame") % team
    rows = pieces[0].shape[1]
    copies = []
    for step, piece in enumerate(pieces):
        start = pl.multiple_of((member + step) % team * rows, rows)
        copies.append((piece, out_hbm.at[:, pl.ds(start, rows), head_width:]))
    run_copies(copies, sems)


def body(queries, keys, values):
    frames_dev, tokens_dev, width = queries.shape
    head_width = width // 2
    score_scale = 1.0 / math.sqrt(head_width)
    count = lax.axis_size("frame")
    team = 2 if count & (count - 1) == 0 and count > 1 else 1
    rows = tokens_dev // team
    dtype = queries.dtype
    hbm = pl.BlockSpec(memory_space=pltpu.HBM)
    vmem = pl.BlockSpec(memory_space=pltpu.VMEM)
    anywhere = pl.BlockSpec(memory_space=pl.ANY)

    def call(kernel, name, flops=1, **rest):
        return pl.pallas_call(
            kernel,
            name=name,
            compiler_params=pltpu.CompilerParams(vmem_limit_bytes=VMEM_LIMIT),
            cost_estimate=pl.CostEstimate(flops=flops, bytes_accessed=1, transcendentals=0),
            **rest,
        )

    def in_vmem(*shape, of=dtype):
        return pltpu.VMEM(shape, of)

    pair, triple = ((size, frames_dev, rows, head_width) for size in (2, 3))
    whole = (frames_dev, tokens_dev, head_width)
    cut = call(
        functools.partial(prep_kernel, team, head_width),
        "prep",
        out_shape=[in_vmem(*pair)] * team
        + [in_vmem(*triple)] * (team - 1)
        + [in_vmem(*pair[1:]), in_vmem(2, *whole), in_vmem(*whole)],
        in_specs=[hbm] * 3,
        out_specs=[vmem] * (2 * team + 2),
        scratch_shapes=[pltpu.SemaphoreType.DMA((5 * team + 1,))],
    )(*(pltpu.with_memory_space_constraint(array, pltpu.HBM) for array in (queries, keys, values)))
    pairs, triples, (query_own, kv_own, query_spatial) = cut[:team], cut[team:-3], cut[-3:]

    def hold(arrays, flops):
        return call(
            lambda *refs: None,
            "hold",
            flops=flops,
            out_shape=[in_vmem(*array.shape) for array in arrays],
            in_specs=[anywhere] * len(arrays),
            out_specs=[anywhere] * len(arrays),
            input_output_aliases={n: n for n in range(len(arrays))},
        )(*arrays)

    def exchange(array, axis, step):
        size = lax.axis_size(axis)
        return lax.ppermute(array, axis, [(i, partner_of(i, step, size)) for i in range(size)])

    others = [exchange(pairs[step % team], "frame", step) for step in range(team, count)]
    others = hold(others, 1000 * 10**6)
    mates = [exchange(triples[step - 1], "frame", step) for step in range(1, team)]
    held = hold([*mates, *others], 1000 * 10**6)
    mates, others = held[: team - 1], held[team - 1 :]
    subs, quarters = lax.axis_size("sub"), lax.axis_size("quarter")
    near = [exchange(kv_own, "sub", step) for step in range(1, subs)]
    across = [exchange(kv_own, "quarter", step) for step in range(1, quarters)]

    strip_out = call(
        functools.partial(temporal_kernel, team, count, len(across), score_scale),
        "temporal",
        out_shape=[in_vmem(*pair[1:])] * team + [in_vmem(*kv_own.shape)] * len(across),
        in_specs=[vmem] * (1 + count) + [anywhere] * len(across),
        out_specs=[vmem] * team + [anywhere] * len(across),
        input_output_aliases={1 + count + n: team + n for n in range(len(across))},
    )(pairs[0], query_own, *mates, *others, *across)
    strip_out, across = strip_out[:team], strip_out[team:]
    returned = [exchange(strip_out[step], "frame", step) for step in range(1, team)]
    late = [exchange(piece, "sub", step) for step in range(1, subs) for piece in across]

    early = [kv_own, *near, *across]
    state = [in_vmem(*whole[:2], size, of=jnp.float32) for size in (1, 1, head_width)]
    running = call(
        functools.partial(first_kernel, score_scale, len(early)),
        "first",
        out_shape=state,
        in_specs=[vmem] * (1 + len(early)),
        out_specs=[vmem] * 3,
    )(query_spatial, *early)

    out = call(
        functools.partial(last_kernel, score_scale, len(late)),
        "last",
        out_shape=jax.ShapeDtypeStruct(queries.shape, dtype),
        in_specs=[vmem] * (4 + len(late)),
        out_specs=hbm,
        scratch_shapes=[pltpu.VMEM(whole, dtype), pltpu.SemaphoreType.DMA((1,))],
    )(query_spatial, *late, *running)

    return call(
        functools.partial(join_kernel, team, head_width),
        "join",
        out_shape=jax.ShapeDtypeStruct(queries.shape, dtype),
        in_specs=[vmem] * team + [hbm],
        out_specs=hbm,
        scratch_shapes=[pltpu.SemaphoreType.DMA((team,))],
        input_output_aliases={team: 0},
    )(strip_out[0], *returned, out)


def solution(mesh):
    spec = P(("groups", "frame"), ("quarter", "sub"), None)
    return jax.shard_map(
        body, mesh=mesh, in_specs=(spec,) * 3, out_specs=spec, check_vma=False
    )
```

```python
import functools
import math

import jax
import jax.numpy as jnp
from jax import lax
from jax.experimental import pallas as pl
from jax.experimental.pallas import tpu as pltpu
from jax.sharding import PartitionSpec as P

STRIP = 16
VMEM_LIMIT = 16 * 1024 * 1024


def partner_of(index, step, count):
    if count & (count - 1) == 0:
        return index ^ step
    return (index + step) % count


def run_copies(copies, sems):
    started = [pltpu.make_async_copy(src, dst, sems.at[n]) for n, (src, dst) in enumerate(copies)]
    for copy in started:
        copy.start()
    for copy in started:
        copy.wait()


def strips_kernel(team, head_width, q_hbm, k_hbm, v_hbm, *refs):
    pairs, triples, sems = refs[:team], refs[team:-1], refs[-1]
    member = lax.axis_index("frame") % team
    rows = pairs[0].shape[2]
    copies = []
    for step in range(team):
        start = pl.multiple_of((member + step) % team * rows, rows)
        cuts = [array.at[:, pl.ds(start, rows), head_width:] for array in (k_hbm, v_hbm, q_hbm)]
        copies += [(cut, pairs[step].at[which]) for which, cut in enumerate(cuts[:2])]
        if step:
            copies += [(cut, triples[step - 1].at[which]) for which, cut in enumerate(cuts)]
    run_copies(copies, sems)


def rest_kernel(team, q_hbm, k_hbm, v_hbm, _, q_own, kv_ref, q_spatial, sems):
    rows, head_width = q_own.shape[1:]
    start = pl.multiple_of(lax.axis_index("frame") % team * rows, rows)
    copies = [(array.at[:, :, :head_width], kv_ref.at[n]) for n, array in enumerate((k_hbm, v_hbm))]
    copies.append((q_hbm.at[:, :, :head_width], q_spatial))
    copies.append((q_hbm.at[:, pl.ds(start, rows), head_width:], q_own))
    run_copies(copies, sems)


def score(query_rows, key_rows, score_scale):
    product = lax.dot_general(
        query_rows, key_rows, (((1,), (1,)), ((), ())), preferred_element_type=jnp.float32
    )
    return product * score_scale


def mix(expo, value_rows):
    return jnp.dot(expo.astype(jnp.bfloat16), value_rows, preferred_element_type=jnp.float32)


def temporal_kernel(team, count, passed, score_scale, *refs):
    own, own_query, mates, others = refs[0], refs[1], refs[2 : 1 + team], refs[1 + team : 1 + count]
    outs = refs[1 + count + passed :][:team]
    frames_dev, rows = own_query.shape[:2]
    cuts = [slice(lower, lower + STRIP) for lower in range(0, rows, STRIP)]

    def gather(parts, cut):
        return jnp.concatenate([part[f, cut] for part in parts for f in range(frames_dev)])

    blocks = [own, *mates, *others]
    queries = [gather([own_query, *(m.at[2] for m in mates)], cut) for cut in cuts]
    keys = [gather([b.at[0] for b in blocks], cut) for cut in cuts]
    values = [gather([b.at[1] for b in blocks], cut) for cut in cuts]
    scores = [score(q, k, score_scale) for q, k in zip(queries, keys)]
    highest = [jnp.max(s, axis=-1, keepdims=True) for s in scores]
    expo = [jnp.exp(s - h) for s, h in zip(scores, highest)]
    totals = [jnp.sum(e, axis=-1, keepdims=True) for e in expo]
    mixed = [mix(e, v) for e, v in zip(expo, values)]
    results = [(m / t).astype(jnp.bfloat16) for m, t in zip(mixed, totals)]
    for cut, result in zip(cuts, results):
        for number, ref in enumerate(outs):
            for frame in range(frames_dev):
                lower = (number * frames_dev + frame) * STRIP
                ref[frame, cut] = result[lower : lower + STRIP]


def first_kernel(score_scale, pieces, q_ref, *refs):
    kvs, (top_ref, total_ref, acc_ref) = refs[:pieces], refs[pieces:]
    for frame in range(q_ref.shape[0]):
        key = jnp.concatenate([kv[0, frame] for kv in kvs])
        value = jnp.concatenate([kv[1, frame] for kv in kvs])
        scores = score(q_ref[frame], key, score_scale)
        highest = jnp.max(scores, axis=-1, keepdims=True)
        expo = jnp.exp(scores - highest)
        top_ref[frame] = highest
        total_ref[frame] = jnp.sum(expo, axis=-1, keepdims=True)
        acc_ref[frame] = mix(expo, value)


def last_kernel(score_scale, pieces, q_ref, *refs):
    kvs, (top_ref, total_ref, acc_ref, out_hbm, o_ref, sems) = refs[:pieces], refs[pieces:]
    head_width = q_ref.shape[-1]
    for frame in range(q_ref.shape[0]):
        key = jnp.concatenate([kv[0, frame] for kv in kvs])
        value = jnp.concatenate([kv[1, frame] for kv in kvs])
        scores = score(q_ref[frame], key, score_scale)
        highest = jnp.maximum(top_ref[frame], jnp.max(scores, axis=-1, keepdims=True))
        expo = jnp.exp(scores - highest)
        factor = jnp.exp(top_ref[frame] - highest)
        total = total_ref[frame] * factor + jnp.sum(expo, axis=-1, keepdims=True)
        o_ref[frame] = ((acc_ref[frame] * factor + mix(expo, value)) / total).astype(jnp.bfloat16)
    run_copies([(o_ref, out_hbm.at[:, :, :head_width])], sems)


def join_kernel(team, head_width, *refs):
    pieces, out_hbm, sems = refs[:team], refs[team + 1], refs[team + 2]
    member = lax.axis_index("frame") % team
    rows = pieces[0].shape[1]
    copies = []
    for step, piece in enumerate(pieces):
        start = pl.multiple_of((member + step) % team * rows, rows)
        copies.append((piece, out_hbm.at[:, pl.ds(start, rows), head_width:]))
    run_copies(copies, sems)


def body(queries, keys, values):
    frames_dev, tokens_dev, width = queries.shape
    head_width = width // 2
    score_scale = 1.0 / math.sqrt(head_width)
    count = lax.axis_size("frame")
    team = 2 if count & (count - 1) == 0 and count > 1 else 1
    rows = tokens_dev // team
    dtype = queries.dtype
    hbm = pl.BlockSpec(memory_space=pltpu.HBM)
    vmem = pl.BlockSpec(memory_space=pltpu.VMEM)
    anywhere = pl.BlockSpec(memory_space=pl.ANY)

    def call(kernel, name, flops=1, **rest):
        return pl.pallas_call(
            kernel,
            name=name,
            compiler_params=pltpu.CompilerParams(vmem_limit_bytes=VMEM_LIMIT),
            cost_estimate=pl.CostEstimate(flops=flops, bytes_accessed=1, transcendentals=0),
            **rest,
        )

    def in_vmem(*shape, of=dtype):
        return pltpu.VMEM(shape, of)

    pair, triple = ((size, frames_dev, rows, head_width) for size in (2, 3))
    whole = (frames_dev, tokens_dev, head_width)
    arrays = [
        pltpu.with_memory_space_constraint(array, pltpu.HBM) for array in (queries, keys, values)
    ]
    cut = call(
        functools.partial(strips_kernel, team, head_width),
        "strips",
        out_shape=[in_vmem(*pair)] * team + [in_vmem(*triple)] * (team - 1),
        in_specs=[hbm] * 3,
        out_specs=[vmem] * (2 * team - 1),
        scratch_shapes=[pltpu.SemaphoreType.DMA((5 * team - 3,))],
    )(*arrays)
    pairs, triples = cut[:team], cut[team:]
    query_own, kv_own, query_spatial = call(
        functools.partial(rest_kernel, team),
        "rest",
        out_shape=[in_vmem(*pair[1:]), in_vmem(2, *whole), in_vmem(*whole)],
        in_specs=[hbm] * 3 + [anywhere],
        out_specs=[vmem] * 3,
        scratch_shapes=[pltpu.SemaphoreType.DMA((4,))],
    )(*arrays, pairs[0])

    def hold(arrays, flops):
        return call(
            lambda *refs: None,
            "hold",
            flops=flops,
            out_shape=[in_vmem(*array.shape) for array in arrays],
            in_specs=[anywhere] * len(arrays),
            out_specs=[anywhere] * len(arrays),
            input_output_aliases={n: n for n in range(len(arrays))},
        )(*arrays)

    def exchange(array, axis, step):
        size = lax.axis_size(axis)
        return lax.ppermute(array, axis, [(i, partner_of(i, step, size)) for i in range(size)])

    waves = [(range(team, team + 1), 1000), ([*range(1, team), *range(team + 1, count)], 1750)]
    arrived = {}
    for steps, mflops in waves:
        for step in steps:
            if step < count:
                block = triples[step - 1] if step < team else pairs[step % team]
                arrived[step] = exchange(block, "frame", step)
        if arrived:
            arrived = dict(zip(arrived, hold(list(arrived.values()), mflops * 10**6)))
    mates, others = ([arrived[n] for n in steps] for steps in (range(1, team), range(team, count)))
    subs, quarters = lax.axis_size("sub"), lax.axis_size("quarter")
    near = [exchange(kv_own, "sub", step) for step in range(1, subs)]
    across = [exchange(kv_own, "quarter", step) for step in range(1, quarters)]

    strip_out = call(
        functools.partial(temporal_kernel, team, count, len(across), score_scale),
        "temporal",
        out_shape=[in_vmem(*pair[1:])] * team + [in_vmem(*kv_own.shape)] * len(across),
        in_specs=[vmem] * (1 + count) + [anywhere] * len(across),
        out_specs=[vmem] * team + [anywhere] * len(across),
        input_output_aliases={1 + count + n: team + n for n in range(len(across))},
    )(pairs[0], query_own, *mates, *others, *across)
    strip_out, across = strip_out[:team], strip_out[team:]
    returned = [exchange(strip_out[step], "frame", step) for step in range(1, team)]
    late = [exchange(piece, "sub", step) for step in range(1, subs) for piece in across]

    early = [kv_own, *near, *across]
    state = [in_vmem(*whole[:2], size, of=jnp.float32) for size in (1, 1, head_width)]
    running = call(
        functools.partial(first_kernel, score_scale, len(early)),
        "first",
        out_shape=state,
        in_specs=[vmem] * (1 + len(early)),
        out_specs=[vmem] * 3,
    )(query_spatial, *early)

    out = call(
        functools.partial(last_kernel, score_scale, len(late)),
        "last",
        out_shape=jax.ShapeDtypeStruct(queries.shape, dtype),
        in_specs=[vmem] * (4 + len(late)),
        out_specs=hbm,
        scratch_shapes=[pltpu.VMEM(whole, dtype), pltpu.SemaphoreType.DMA((1,))],
    )(query_spatial, *late, *running)

    return call(
        functools.partial(join_kernel, team, head_width),
        "join",
        out_shape=jax.ShapeDtypeStruct(queries.shape, dtype),
        in_specs=[vmem] * team + [hbm],
        out_specs=hbm,
        scratch_shapes=[pltpu.SemaphoreType.DMA((team,))],
        input_output_aliases={team: 0},
    )(strip_out[0], *returned, out)


def solution(mesh):
    spec = P(("groups", "frame"), ("quarter", "sub"), None)
    return jax.shard_map(
        body, mesh=mesh, in_specs=(spec,) * 3, out_specs=spec, check_vma=False
    )
```

```python
import functools
import math

import jax
import jax.numpy as jnp
from jax import lax
from jax.experimental import pallas as pl
from jax.experimental.pallas import tpu as pltpu
from jax.sharding import PartitionSpec as P

STRIP = 16
SHARE = 8
VMEM_LIMIT = 16 * 1024 * 1024


def partner_of(index, step, count):
    if count & (count - 1) == 0:
        return index ^ step
    return (index + step) % count


def run_copies(copies, sems):
    started = [pltpu.make_async_copy(src, dst, sems.at[n]) for n, (src, dst) in enumerate(copies)]
    for copy in started:
        copy.start()
    for copy in started:
        copy.wait()


def strips_kernel(team, homed, head_width, q_hbm, k_hbm, v_hbm, *refs):
    pairs, mates, sems = refs[:team], refs[team:-1], refs[-1]
    member = lax.axis_index("frame") % team
    free = k_hbm.shape[1] - team * homed
    copies = []
    for step in range(team):
        start = pl.multiple_of((member + step) % team * homed, STRIP)
        cuts = [array.at[:, pl.ds(start, homed), head_width:] for array in (k_hbm, v_hbm, q_hbm)]
        copies += [(cut, pairs[step].at[which]) for which, cut in enumerate(cuts[:2])]
        if step:
            mate = mates[step - 1]
            copies += [(cut, mate.at[:, pl.ds(n * homed, homed)]) for n, cut in enumerate(cuts)]
            if free:
                for n, array in enumerate((k_hbm, v_hbm)):
                    cut = array.at[:, team * homed :, head_width:]
                    copies.append((cut, mate.at[:, pl.ds(3 * homed + n * free, free)]))
    run_copies(copies, sems)


def rest_kernel(team, homed, q_hbm, k_hbm, v_hbm, _, q_own, kv_ref, q_spatial, *refs):
    sems, head_width = refs[-1], q_spatial.shape[2]
    start = pl.multiple_of(lax.axis_index("frame") % team * homed, STRIP)
    copies = [(array.at[:, :, :head_width], kv_ref.at[n]) for n, array in enumerate((k_hbm, v_hbm))]
    copies.append((q_hbm.at[:, :, :head_width], q_spatial))
    copies.append((q_hbm.at[:, pl.ds(start, homed), head_width:], q_own))
    if len(refs) > 1:
        for n, array in enumerate((k_hbm, v_hbm, q_hbm)):
            dst = refs[1] if n == 2 else refs[0].at[n]
            copies.append((array.at[:, team * homed :, head_width:], dst))
    run_copies(copies, sems)


def score(query_rows, key_rows, score_scale):
    product = lax.dot_general(
        query_rows, key_rows, (((1,), (1,)), ((), ())), preferred_element_type=jnp.float32
    )
    return product * score_scale


def mix(expo, value_rows):
    return jnp.dot(expo.astype(jnp.bfloat16), value_rows, preferred_element_type=jnp.float32)


def attend_strips(queries, keys, values, outs, score_scale):
    frames_dev, rows = outs[0].shape[:2]
    cuts = [slice(lower, lower + STRIP) for lower in range(0, rows, STRIP)]

    def gather(parts, cut):
        return jnp.concatenate([part[f, cut] for part in parts for f in range(frames_dev)])

    scores = [score(gather(queries, cut), gather(keys, cut), score_scale) for cut in cuts]
    highest = [jnp.max(s, axis=-1, keepdims=True) for s in scores]
    expo = [jnp.exp(s - h) for s, h in zip(scores, highest)]
    totals = [jnp.sum(e, axis=-1, keepdims=True) for e in expo]
    mixed = [mix(e, gather(values, cut)) for e, cut in zip(expo, cuts)]
    results = [(m / t).astype(jnp.bfloat16) for m, t in zip(mixed, totals)]
    for cut, result in zip(cuts, results):
        for number, ref in enumerate(outs):
            for frame in range(frames_dev):
                lower = (number * frames_dev + frame) * STRIP
                ref[frame, cut] = result[lower : lower + STRIP]


def homed_kernel(team, others, passed, score_scale, own, query, *refs):
    mates, others = refs[: team - 1], refs[team - 1 : team - 1 + others]
    outs = refs[len(mates) + len(others) + passed :][:team]
    homed = query.shape[1]

    def part(which):
        return [mate.at[:, pl.ds(which * homed, homed)] for mate in mates]

    keys, values = (
        [own.at[n], *part(n), *(block.at[n] for block in others)] for n in range(2)
    )
    attend_strips([query, *part(2)], keys, values, outs, score_scale)


def pack_kernel(team, homed, arrived, own, *refs):
    mates, (packed, sems) = refs[: team - 1], (refs[-2], refs[-1])
    free = own.shape[2]
    copies = [(own, packed.at[0])]
    for number, mate in enumerate(mates):
        for n in range(2):
            src = mate.at[:, pl.ds(3 * homed + n * free, free)]
            copies.append((src, packed.at[1 + number, n]))
    run_copies(copies, sems)


def free_kernel(team, score_scale, query, *refs):
    packs, out = refs[:-1], refs[-1]
    keys, values = ([p.at[m, n] for p in packs for m in range(team)] for n in range(2))
    attend_strips([query], keys, values, [out], score_scale)


def first_kernel(score_scale, pieces, q_ref, *refs):
    kvs, (top_ref, total_ref, acc_ref) = refs[:pieces], refs[pieces:]
    for frame in range(q_ref.shape[0]):
        key = jnp.concatenate([kv[0, frame] for kv in kvs])
        value = jnp.concatenate([kv[1, frame] for kv in kvs])
        scores = score(q_ref[frame], key, score_scale)
        highest = jnp.max(scores, axis=-1, keepdims=True)
        expo = jnp.exp(scores - highest)
        top_ref[frame] = highest
        total_ref[frame] = jnp.sum(expo, axis=-1, keepdims=True)
        acc_ref[frame] = mix(expo, value)


def last_kernel(score_scale, pieces, q_ref, *refs):
    kvs, (top_ref, total_ref, acc_ref, out_hbm, o_ref, sems) = refs[:pieces], refs[pieces:]
    head_width = q_ref.shape[-1]
    for frame in range(q_ref.shape[0]):
        key = jnp.concatenate([kv[0, frame] for kv in kvs])
        value = jnp.concatenate([kv[1, frame] for kv in kvs])
        scores = score(q_ref[frame], key, score_scale)
        highest = jnp.maximum(top_ref[frame], jnp.max(scores, axis=-1, keepdims=True))
        expo = jnp.exp(scores - highest)
        factor = jnp.exp(top_ref[frame] - highest)
        total = total_ref[frame] * factor + jnp.sum(expo, axis=-1, keepdims=True)
        o_ref[frame] = ((acc_ref[frame] * factor + mix(expo, value)) / total).astype(jnp.bfloat16)
    run_copies([(o_ref, out_hbm.at[:, :, :head_width])], sems)


def join_kernel(team, homed, head_width, *refs):
    pieces, out_hbm, sems = refs[:-3], refs[-2], refs[-1]
    member = lax.axis_index("frame") % team
    copies = []
    for step, piece in enumerate(pieces):
        start, rows = team * homed, piece.shape[1]
        if step < team:
            start = pl.multiple_of((member + step) % team * homed, STRIP)
        copies.append((piece, out_hbm.at[:, pl.ds(start, rows), head_width:]))
    run_copies(copies, sems)


def body(queries, keys, values):
    frames_dev, tokens_dev, width = queries.shape
    head_width = width // 2
    score_scale = 1.0 / math.sqrt(head_width)
    count = lax.axis_size("frame")
    subs, quarters = lax.axis_size("sub"), lax.axis_size("quarter")
    team = 2 if count & (count - 1) == 0 and count > 1 else 1
    strips = tokens_dev // STRIP
    homed = (strips - strips // SHARE) // team * STRIP if team > 1 else tokens_dev
    free = tokens_dev - team * homed
    dtype = queries.dtype
    hbm = pl.BlockSpec(memory_space=pltpu.HBM)
    vmem = pl.BlockSpec(memory_space=pltpu.VMEM)
    anywhere = pl.BlockSpec(memory_space=pl.ANY)

    def call(kernel, name, mflops=0, **rest):
        return pl.pallas_call(
            kernel,
            name=name,
            compiler_params=pltpu.CompilerParams(vmem_limit_bytes=VMEM_LIMIT),
            cost_estimate=pl.CostEstimate(
                flops=mflops * 10**6 + 1, bytes_accessed=1, transcendentals=0
            ),
            **rest,
        )

    def in_vmem(*shape, of=dtype):
        return pltpu.VMEM(shape, of)

    block, spare, whole = (
        (frames_dev, rows, head_width) for rows in (homed, free, tokens_dev)
    )
    arrays = [
        pltpu.with_memory_space_constraint(array, pltpu.HBM) for array in (queries, keys, values)
    ]
    cut = call(
        functools.partial(strips_kernel, team, homed, head_width),
        "strips",
        out_shape=[in_vmem(2, *block)] * team
        + [in_vmem(frames_dev, 3 * homed + 2 * free, head_width)] * (team - 1),
        in_specs=[hbm] * 3,
        out_specs=[vmem] * (2 * team - 1),
        scratch_shapes=[pltpu.SemaphoreType.DMA((7 * team,))],
    )(*arrays)
    pairs, triples = cut[:team], cut[team:]
    spares = [in_vmem(2, *spare), in_vmem(*spare)] if free else []
    query_own, kv_own, query_spatial, *spares = call(
        functools.partial(rest_kernel, team, homed),
        "rest",
        out_shape=[in_vmem(*block), in_vmem(2, *whole), in_vmem(*whole), *spares],
        in_specs=[hbm] * 3 + [anywhere],
        out_specs=[vmem] * (3 + len(spares)),
        scratch_shapes=[pltpu.SemaphoreType.DMA((7,))],
    )(*arrays, pairs[0])

    def hold(arrays, mflops, far=()):
        total = len(arrays) + len(far)
        return call(
            lambda *refs: None,
            "hold",
            mflops=mflops,
            out_shape=[in_vmem(*array.shape, of=array.dtype) for array in arrays]
            + [jax.ShapeDtypeStruct(array.shape, dtype) for array in far],
            in_specs=[anywhere] * len(arrays) + [hbm] * len(far),
            out_specs=[anywhere] * len(arrays) + [hbm] * len(far),
            input_output_aliases={n: n for n in range(total)},
        )(*arrays, *far)

    def exchange(array, axis, step):
        size = lax.axis_size(axis)
        return lax.ppermute(array, axis, [(i, partner_of(i, step, size)) for i in range(size)])

    cross = {step: exchange(pairs[step % team], "frame", step) for step in range(team, count)}
    mates = [exchange(triples[step - 1], "frame", step) for step in range(1, team)]
    across = [exchange(kv_own, "quarter", step) for step in range(1, quarters)]
    near = [exchange(kv_own, "sub", step) for step in range(1, subs)]
    if cross:
        [cross[team]] = hold([cross[team]], 1150)
    if free:
        gate = [cross[team]] if cross else []
        *gate, packed = call(
            functools.partial(pack_kernel, team, homed, 0),
            "pack",
            mflops=0,
            out_shape=[in_vmem(*g.shape) for g in gate] + [in_vmem(team, 2, *spare)],
            in_specs=[vmem] * team + [anywhere] * len(gate),
            out_specs=[anywhere] * len(gate) + [vmem],
            scratch_shapes=[pltpu.SemaphoreType.DMA((1 + 2 * (team - 1),))],
            input_output_aliases={team: 0} if gate else {},
        )(spares[0], *mates, *gate)
        if gate:
            [cross[team]] = gate
        spread = [exchange(packed, "frame", step) for step in range(team, count, team)]
    held = hold([*mates, *cross.values()], 1900)
    mates, others = held[: team - 1], held[team - 1 :]
    across = hold(across, 100)

    strip_out = call(
        functools.partial(homed_kernel, team, len(others), 0, score_scale),
        "homed",
        mflops=0,
        out_shape=[in_vmem(*block)] * team,
        in_specs=[vmem] * (1 + count),
        out_specs=[vmem] * team,
    )(pairs[0], query_own, *mates, *others)
    returned = [exchange(strip_out[step], "frame", step) for step in range(1, team)]

    early = [kv_own, *near, *across]
    late = [exchange(piece, "sub", step) for step in range(1, subs) for piece in across]
    running = call(
        functools.partial(first_kernel, score_scale, len(early)),
        "first",
        out_shape=[in_vmem(*whole[:2], size, of=jnp.float32) for size in (1, 1, head_width)],
        in_specs=[vmem] * (1 + len(early)),
        out_specs=[vmem] * 3,
    )(query_spatial, *early)
    if free:
        held = hold([*spread, *running], 4000)
        spread, running = held[: len(spread)], held[len(spread) :]
    out = call(
        functools.partial(last_kernel, score_scale, len(late)),
        "last",
        out_shape=jax.ShapeDtypeStruct(queries.shape, dtype),
        in_specs=[vmem] * (4 + len(late)),
        out_specs=hbm,
        scratch_shapes=[pltpu.VMEM(whole, dtype), pltpu.SemaphoreType.DMA((1,))],
    )(query_spatial, *late, *running)

    pieces = [strip_out[0], *returned]
    if free:
        pieces.append(
            call(
                functools.partial(free_kernel, team, score_scale),
                "free",
                out_shape=in_vmem(*spare),
                in_specs=[vmem] * (2 + len(spread)),
                out_specs=vmem,
            )(spares[1], packed, *spread)
        )
    return call(
        functools.partial(join_kernel, team, homed, head_width),
        "join",
        out_shape=jax.ShapeDtypeStruct(queries.shape, dtype),
        in_specs=[vmem] * len(pieces) + [hbm],
        out_specs=hbm,
        scratch_shapes=[pltpu.SemaphoreType.DMA((len(pieces),))],
        input_output_aliases={len(pieces): 0},
    )(*pieces, out)


def solution(mesh):
    spec = P(("groups", "frame"), ("quarter", "sub"), None)
    return jax.shard_map(
        body, mesh=mesh, in_specs=(spec,) * 3, out_specs=spec, check_vma=False
    )
```

```python
import functools
import math

import jax
import jax.numpy as jnp
from jax import lax
from jax.experimental import pallas as pl
from jax.experimental.pallas import tpu as pltpu
from jax.sharding import PartitionSpec as P

STRIP = 16
SHARE = 8
VMEM_LIMIT = 16 * 1024 * 1024


def partner_of(index, step, count):
    if count & (count - 1) == 0:
        return index ^ step
    return (index + step) % count


def run_copies(copies, sems):
    started = [pltpu.make_async_copy(src, dst, sems.at[n]) for n, (src, dst) in enumerate(copies)]
    for copy in started:
        copy.start()
    for copy in started:
        copy.wait()


def first_row(member, homed, free):
    return pl.multiple_of(member * (homed + free), STRIP)


def strips_kernel(team, free, head_width, q_hbm, k_hbm, v_hbm, *refs):
    pairs, mates, sems = refs[:team], refs[team:-1], refs[-1]
    homed = pairs[0].shape[2]
    span = homed + free
    copies = []
    for step in range(team):
        member = (lax.axis_index("frame") + step) % team
        start = first_row(member, homed, free)
        for n, array in enumerate((k_hbm, v_hbm)):
            copies.append((array.at[:, pl.ds(start, homed), head_width:], pairs[step].at[n]))
        if step:
            mate, wide = mates[step - 1], pl.multiple_of(member * homed, STRIP)
            for n, array in enumerate((k_hbm, v_hbm)):
                cut = array.at[:, pl.ds(wide, span), head_width:]
                copies.append((cut, mate.at[:, pl.ds(n * span, span)]))
            cut = q_hbm.at[:, pl.ds(start, homed), head_width:]
            copies.append((cut, mate.at[:, pl.ds(2 * span, homed)]))
    run_copies(copies, sems)


def rest_kernel(team, free, q_hbm, k_hbm, v_hbm, _, q_own, kv_ref, q_spatial, *refs):
    sems, head_width, homed = refs[-1], q_spatial.shape[2], q_own.shape[1]
    start = first_row(lax.axis_index("frame") % team, homed, free)
    copies = [(array.at[:, :, :head_width], kv_ref.at[n]) for n, array in enumerate((k_hbm, v_hbm))]
    copies.append((q_hbm.at[:, :, :head_width], q_spatial))
    copies.append((q_hbm.at[:, pl.ds(start, homed), head_width:], q_own))
    if free:
        for n, array in enumerate((k_hbm, v_hbm, q_hbm)):
            dst = refs[1] if n == 2 else refs[0].at[n]
            copies.append((array.at[:, homed : homed + free, head_width:], dst))
    run_copies(copies, sems)


def score(query_rows, key_rows, score_scale):
    product = lax.dot_general(
        query_rows, key_rows, (((1,), (1,)), ((), ())), preferred_element_type=jnp.float32
    )
    return product * score_scale


def mix(expo, value_rows):
    return jnp.dot(expo.astype(jnp.bfloat16), value_rows, preferred_element_type=jnp.float32)


def attend_strips(queries, keys, values, outs, score_scale):
    frames_dev, rows = outs[0].shape[:2]
    cuts = [slice(lower, lower + STRIP) for lower in range(0, rows, STRIP)]

    def gather(parts, cut):
        return jnp.concatenate([part[f, cut] for part in parts for f in range(frames_dev)])

    scores = []
    for at in range(0, len(cuts), 2):
        query, key = ([gather(parts, cut) for cut in cuts[at : at + 2]] for parts in (queries, keys))
        both = score(jnp.concatenate(query), jnp.concatenate(key), score_scale)
        q, k = query[0].shape[0], key[0].shape[0]
        scores += [both[n * q : (n + 1) * q, n * k : (n + 1) * k] for n in range(len(query))]
    highest = [jnp.max(s, axis=-1, keepdims=True) for s in scores]
    expo = [jnp.exp(s - h) for s, h in zip(scores, highest)]
    totals = [jnp.sum(e, axis=-1, keepdims=True) for e in expo]
    mixed = [mix(e, gather(values, cut)) for e, cut in zip(expo, cuts)]
    results = [(m / t).astype(jnp.bfloat16) for m, t in zip(mixed, totals)]
    for cut, result in zip(cuts, results):
        for number, ref in enumerate(outs):
            for frame in range(frames_dev):
                lower = (number * frames_dev + frame) * STRIP
                ref[frame, cut] = result[lower : lower + STRIP]


def homed_kernel(team, others, free, score_scale, own, query, *refs):
    mates, others, outs = refs[: team - 1], refs[team - 1 : team - 1 + others], refs[-team:]
    homed = query.shape[1]
    span, skip = homed + free, lax.axis_index("frame") % team * free

    def part(start):
        return [mate.at[:, pl.ds(pl.multiple_of(start, STRIP), homed)] for mate in mates]

    keys, values = (
        [own.at[n], *part(n * span + skip), *(block.at[n] for block in others)] for n in range(2)
    )
    attend_strips([query, *part(2 * span)], keys, values, outs, score_scale)


def pack_kernel(team, homed, own, *refs):
    mates, packed, sems = refs[: team - 1], refs[-2], refs[-1]
    free = own.shape[2]
    skip = (team - 1 - lax.axis_index("frame") % team) * homed
    copies = [(own, packed.at[0])]
    for number, mate in enumerate(mates):
        for n in range(2):
            start = pl.multiple_of(n * (homed + free) + skip, STRIP)
            copies.append((mate.at[:, pl.ds(start, free)], packed.at[1 + number, n]))
    run_copies(copies, sems)


def free_kernel(team, score_scale, query, *refs):
    packs, out = refs[:-1], refs[-1]
    keys, values = ([p.at[m, n] for p in packs for m in range(team)] for n in range(2))
    attend_strips([query], keys, values, [out], score_scale)


def first_kernel(score_scale, pieces, q_ref, *refs):
    kvs, (top_ref, total_ref, acc_ref) = refs[:pieces], refs[pieces:]
    for frame in range(q_ref.shape[0]):
        key = jnp.concatenate([kv[0, frame] for kv in kvs])
        value = jnp.concatenate([kv[1, frame] for kv in kvs])
        scores = score(q_ref[frame], key, score_scale)
        highest = jnp.max(scores, axis=-1, keepdims=True)
        expo = jnp.exp(scores - highest)
        top_ref[frame] = highest
        total_ref[frame] = jnp.sum(expo, axis=-1, keepdims=True)
        acc_ref[frame] = mix(expo, value)


def last_kernel(score_scale, pieces, team, q_ref, *refs):
    kvs, (top_ref, total_ref, acc_ref), refs = refs[:pieces], refs[pieces : pieces + 3], refs[pieces + 3 :]
    ready, (out_hbm, o_ref, sems) = refs[:-3], refs[-3:]
    frames, _, head_width = q_ref.shape
    homed, free = ready[0].shape[1], sum(ref.shape[1] for ref in ready[1:])
    starts = [first_row(lax.axis_index("frame") % team, homed, free), homed]
    copies = []

    def send(src, dst):
        copies.append(pltpu.make_async_copy(src, dst, sems.at[len(copies)]))
        copies[-1].start()

    for start, ref in zip(starts, ready):
        send(ref, out_hbm.at[:, pl.ds(start, ref.shape[1]), head_width:])
    for frame in range(frames):
        key = jnp.concatenate([kv[0, frame] for kv in kvs])
        value = jnp.concatenate([kv[1, frame] for kv in kvs])
        scores = score(q_ref[frame], key, score_scale)
        highest = jnp.maximum(top_ref[frame], jnp.max(scores, axis=-1, keepdims=True))
        expo = jnp.exp(scores - highest)
        factor = jnp.exp(top_ref[frame] - highest)
        total = total_ref[frame] * factor + jnp.sum(expo, axis=-1, keepdims=True)
        o_ref[frame] = ((acc_ref[frame] * factor + mix(expo, value)) / total).astype(jnp.bfloat16)
        send(o_ref.at[frame], out_hbm.at[frame, :, :head_width])
    for copy in copies:
        copy.wait()


def join_kernel(team, free, head_width, *refs):
    pieces, out_hbm, sems = refs[:-3], refs[-2], refs[-1]
    copies = []
    for number, piece in enumerate(pieces):
        rows = piece.shape[1]
        start = first_row((lax.axis_index("frame") + 1 + number) % team, rows, free)
        copies.append((piece, out_hbm.at[:, pl.ds(start, rows), head_width:]))
    run_copies(copies, sems)


def body(queries, keys, values):
    frames_dev, tokens_dev, width = queries.shape
    head_width = width // 2
    score_scale = 1.0 / math.sqrt(head_width)
    count = lax.axis_size("frame")
    subs, quarters = lax.axis_size("sub"), lax.axis_size("quarter")
    team = 2 if count & (count - 1) == 0 and count > 1 else 1
    strips = tokens_dev // STRIP
    homed = (strips - strips // SHARE) // team * STRIP if team > 1 else tokens_dev
    free = tokens_dev - team * homed
    dtype = queries.dtype
    hbm = pl.BlockSpec(memory_space=pltpu.HBM)
    vmem = pl.BlockSpec(memory_space=pltpu.VMEM)
    anywhere = pl.BlockSpec(memory_space=pl.ANY)

    def call(kernel, name, mflops=0, **rest):
        return pl.pallas_call(
            kernel,
            name=name,
            compiler_params=pltpu.CompilerParams(vmem_limit_bytes=VMEM_LIMIT),
            cost_estimate=pl.CostEstimate(
                flops=mflops * 10**6 + 1, bytes_accessed=1, transcendentals=0
            ),
            **rest,
        )

    def in_vmem(*shape, of=dtype):
        return pltpu.VMEM(shape, of)

    block, spare, whole = (
        (frames_dev, rows, head_width) for rows in (homed, free, tokens_dev)
    )
    arrays = [
        pltpu.with_memory_space_constraint(array, pltpu.HBM) for array in (queries, keys, values)
    ]
    cut = call(
        functools.partial(strips_kernel, team, free, head_width),
        "strips",
        out_shape=[in_vmem(2, *block)] * team
        + [in_vmem(frames_dev, 3 * homed + 2 * free, head_width)] * (team - 1),
        in_specs=[hbm] * 3,
        out_specs=[vmem] * (2 * team - 1),
        scratch_shapes=[pltpu.SemaphoreType.DMA((5 * team - 3,))],
    )(*arrays)
    pairs, triples = cut[:team], cut[team:]
    spares = [in_vmem(2, *spare), in_vmem(*spare)] if free else []
    query_own, kv_own, query_spatial, *spares = call(
        functools.partial(rest_kernel, team, free),
        "rest",
        out_shape=[in_vmem(*block), in_vmem(2, *whole), in_vmem(*whole), *spares],
        in_specs=[hbm] * 3 + [anywhere],
        out_specs=[vmem] * (3 + len(spares)),
        scratch_shapes=[pltpu.SemaphoreType.DMA((7,))],
    )(*arrays, pairs[0])

    def hold(arrays, mflops, far=()):
        total = len(arrays) + len(far)
        return call(
            lambda *refs: None,
            "hold",
            mflops=mflops,
            out_shape=[in_vmem(*array.shape, of=array.dtype) for array in arrays]
            + [jax.ShapeDtypeStruct(array.shape, dtype) for array in far],
            in_specs=[anywhere] * len(arrays) + [hbm] * len(far),
            out_specs=[anywhere] * len(arrays) + [hbm] * len(far),
            input_output_aliases={n: n for n in range(total)},
        )(*arrays, *far)

    def exchange(array, axis, step):
        size = lax.axis_size(axis)
        return lax.ppermute(array, axis, [(i, partner_of(i, step, size)) for i in range(size)])

    cross = {step: exchange(pairs[step % team], "frame", step) for step in range(team, count)}
    mates = [exchange(triples[step - 1], "frame", step) for step in range(1, team)]
    across = [exchange(kv_own, "quarter", step) for step in range(1, quarters)]
    near = [exchange(kv_own, "sub", step) for step in range(1, subs)]
    if cross:
        [cross[team]] = hold([cross[team]], 1150)
    if free:
        packed = call(
            functools.partial(pack_kernel, team, homed),
            "pack",
            out_shape=in_vmem(team, 2, *spare),
            in_specs=[vmem] * team,
            out_specs=vmem,
            scratch_shapes=[pltpu.SemaphoreType.DMA((2 * team - 1,))],
        )(spares[0], *mates)
        spread = [exchange(packed, "frame", step) for step in range(team, count, team)]
    held = hold([*mates, *cross.values()], 1900)
    mates, others = held[: team - 1], held[team - 1 :]
    across = hold(across, 100)

    strip_out = call(
        functools.partial(homed_kernel, team, len(others), free, score_scale),
        "homed",
        mflops=0,
        out_shape=[in_vmem(*block)] * team,
        in_specs=[vmem] * (1 + count),
        out_specs=[vmem] * team,
    )(pairs[0], query_own, *mates, *others)
    returned = [exchange(strip_out[step], "frame", step) for step in range(1, team)]

    early = [kv_own, *near, *across]
    late = [exchange(piece, "sub", step) for step in range(1, subs) for piece in across]
    running = call(
        functools.partial(first_kernel, score_scale, len(early)),
        "first",
        out_shape=[in_vmem(*whole[:2], size, of=jnp.float32) for size in (1, 1, head_width)],
        in_specs=[vmem] * (1 + len(early)),
        out_specs=[vmem] * 3,
    )(query_spatial, *early)
    if free:
        held = hold([*spread, *running], 4000)
        spread, running = held[: len(spread)], held[len(spread) :]
    ready = [strip_out[0]]
    if free:
        ready.append(
            call(
                functools.partial(free_kernel, team, score_scale),
                "free",
                out_shape=in_vmem(*spare),
                in_specs=[vmem] * (2 + len(spread)),
                out_specs=vmem,
            )(spares[1], packed, *spread)
        )
    out = call(
        functools.partial(last_kernel, score_scale, len(late), team),
        "last",
        out_shape=jax.ShapeDtypeStruct(queries.shape, dtype),
        in_specs=[vmem] * (4 + len(late) + len(ready)),
        out_specs=hbm,
        scratch_shapes=[
            pltpu.VMEM(whole, dtype),
            pltpu.SemaphoreType.DMA((frames_dev + len(ready),)),
        ],
    )(query_spatial, *late, *running, *ready)

    return call(
        functools.partial(join_kernel, team, free, head_width),
        "join",
        out_shape=jax.ShapeDtypeStruct(queries.shape, dtype),
        in_specs=[vmem] * len(returned) + [hbm],
        out_specs=hbm,
        scratch_shapes=[pltpu.SemaphoreType.DMA((max(1, len(returned)),))],
        input_output_aliases={len(returned): 0},
    )(*returned, out)


def solution(mesh):
    spec = P(("groups", "frame"), ("quarter", "sub"), None)
    return jax.shard_map(
        body, mesh=mesh, in_specs=(spec,) * 3, out_specs=spec, check_vma=False
    )
```

```python
import functools
import math

import jax
import jax.numpy as jnp
from jax import lax
from jax.experimental import pallas as pl
from jax.experimental.pallas import tpu as pltpu
from jax.sharding import PartitionSpec as P

STRIP = 16
SHARE = 8
VMEM_LIMIT = 16 * 1024 * 1024


def partner_of(index, step, count):
    if count & (count - 1) == 0:
        return index ^ step
    return (index + step) % count


def run_copies(copies, sems):
    started = [pltpu.make_async_copy(src, dst, sems.at[n]) for n, (src, dst) in enumerate(copies)]
    for copy in started:
        copy.start()
    for copy in started:
        copy.wait()


def first_row(member, homed, free):
    return pl.multiple_of(member * (homed + free), STRIP)


def strips_kernel(team, free, head_width, q_hbm, k_hbm, v_hbm, *refs):
    pairs, mates, sems = refs[:team], refs[team:-1], refs[-1]
    homed = pairs[0].shape[2]
    span = homed + free
    copies = []
    for step in range(team):
        member = (lax.axis_index("frame") + step) % team
        start = first_row(member, homed, free)
        for n, array in enumerate((k_hbm, v_hbm)):
            copies.append((array.at[:, pl.ds(start, homed), head_width:], pairs[step].at[n]))
        if step:
            mate, wide = mates[step - 1], pl.multiple_of(member * homed, STRIP)
            for n, array in enumerate((k_hbm, v_hbm)):
                cut = array.at[:, pl.ds(wide, span), head_width:]
                copies.append((cut, mate.at[:, pl.ds(n * span, span)]))
            cut = q_hbm.at[:, pl.ds(start, homed), head_width:]
            copies.append((cut, mate.at[:, pl.ds(2 * span, homed)]))
    run_copies(copies, sems)


def rest_kernel(team, free, q_hbm, k_hbm, v_hbm, _, q_own, kv_ref, q_spatial, *refs):
    sems, head_width, homed = refs[-1], q_spatial.shape[2], q_own.shape[1]
    start = first_row(lax.axis_index("frame") % team, homed, free)
    copies = [(array.at[:, :, :head_width], kv_ref.at[n]) for n, array in enumerate((k_hbm, v_hbm))]
    copies.append((q_hbm.at[:, :, :head_width], q_spatial))
    copies.append((q_hbm.at[:, pl.ds(start, homed), head_width:], q_own))
    if free:
        for n, array in enumerate((k_hbm, v_hbm, q_hbm)):
            dst = refs[1] if n == 2 else refs[0].at[n]
            copies.append((array.at[:, homed : homed + free, head_width:], dst))
    run_copies(copies, sems)


def score(query_rows, key_rows, score_scale):
    product = lax.dot_general(
        query_rows, key_rows, (((1,), (1,)), ((), ())), preferred_element_type=jnp.float32
    )
    return product * score_scale


def mix(expo, value_rows):
    return jnp.dot(expo.astype(jnp.bfloat16), value_rows, preferred_element_type=jnp.float32)


def attend_strips(queries, keys, values, outs, score_scale):
    frames_dev, rows = outs[0].shape[:2]
    cuts = [slice(lower, lower + STRIP) for lower in range(0, rows, STRIP)]

    def gather(parts, cut):
        return jnp.concatenate([part[f, cut] for part in parts for f in range(frames_dev)])

    scores = []
    for at in range(0, len(cuts), 2):
        query, key = ([gather(parts, cut) for cut in cuts[at : at + 2]] for parts in (queries, keys))
        both = score(jnp.concatenate(query), jnp.concatenate(key), score_scale)
        q, k = query[0].shape[0], key[0].shape[0]
        scores += [both[n * q : (n + 1) * q, n * k : (n + 1) * k] for n in range(len(query))]
    highest = [jnp.max(s, axis=-1, keepdims=True) for s in scores]
    expo = [jnp.exp(s - h) for s, h in zip(scores, highest)]
    totals = [jnp.sum(e, axis=-1, keepdims=True) for e in expo]
    mixed = [mix(e, gather(values, cut)) for e, cut in zip(expo, cuts)]
    results = [(m / t).astype(jnp.bfloat16) for m, t in zip(mixed, totals)]
    for cut, result in zip(cuts, results):
        for number, ref in enumerate(outs):
            for frame in range(frames_dev):
                lower = (number * frames_dev + frame) * STRIP
                ref[frame, cut] = result[lower : lower + STRIP]


def homed_kernel(team, others, free, score_scale, own, query, *refs):
    mates, others, outs = refs[: team - 1], refs[team - 1 : team - 1 + others], refs[-team:]
    homed = query.shape[1]
    span, skip = homed + free, lax.axis_index("frame") % team * free

    def part(start):
        return [mate.at[:, pl.ds(pl.multiple_of(start, STRIP), homed)] for mate in mates]

    keys, values = (
        [own.at[n], *part(n * span + skip), *(block.at[n] for block in others)] for n in range(2)
    )
    attend_strips([query, *part(2 * span)], keys, values, outs, score_scale)


def pack_kernel(team, homed, own, *refs):
    mates, packed, sems = refs[: team - 1], refs[-2], refs[-1]
    free = own.shape[2]
    skip = (team - 1 - lax.axis_index("frame") % team) * homed
    copies = [(own, packed.at[0])]
    for number, mate in enumerate(mates):
        for n in range(2):
            start = pl.multiple_of(n * (homed + free) + skip, STRIP)
            copies.append((mate.at[:, pl.ds(start, free)], packed.at[1 + number, n]))
    run_copies(copies, sems)


def free_kernel(team, score_scale, query, *refs):
    packs, out = refs[:-1], refs[-1]
    keys, values = ([p.at[m, n] for p in packs for m in range(team)] for n in range(2))
    attend_strips([query], keys, values, [out], score_scale)


def first_kernel(score_scale, pieces, q_ref, *refs):
    kvs, (top_ref, total_ref, acc_ref) = refs[:pieces], refs[pieces:]
    for frame in range(q_ref.shape[0]):
        key = jnp.concatenate([kv[0, frame] for kv in kvs])
        value = jnp.concatenate([kv[1, frame] for kv in kvs])
        scores = score(q_ref[frame], key, score_scale)
        highest = jnp.max(scores, axis=-1, keepdims=True)
        expo = jnp.exp(scores - highest)
        top_ref[frame] = highest
        total_ref[frame] = jnp.sum(expo, axis=-1, keepdims=True)
        acc_ref[frame] = mix(expo, value)


def last_kernel(score_scale, pieces, q_ref, *refs):
    kvs, (top_ref, total_ref, acc_ref, o_ref) = refs[:pieces], refs[pieces:]
    for frame in range(q_ref.shape[0]):
        key = jnp.concatenate([kv[0, frame] for kv in kvs])
        value = jnp.concatenate([kv[1, frame] for kv in kvs])
        scores = score(q_ref[frame], key, score_scale)
        highest = jnp.maximum(top_ref[frame], jnp.max(scores, axis=-1, keepdims=True))
        expo = jnp.exp(scores - highest)
        factor = jnp.exp(top_ref[frame] - highest)
        total = total_ref[frame] * factor + jnp.sum(expo, axis=-1, keepdims=True)
        o_ref[frame] = ((acc_ref[frame] * factor + mix(expo, value)) / total).astype(jnp.bfloat16)


def join_kernel(team, free, spatial, *refs):
    pieces, out_hbm, sems = refs[:-2], refs[-2], refs[-1]
    head_width = spatial.shape[2]
    copies = [(spatial, out_hbm.at[:, :, :head_width])]
    for number, piece in enumerate(pieces):
        rows = piece.shape[1]
        if number < team:
            start = first_row((lax.axis_index("frame") + number) % team, rows, free)
        else:
            start = pieces[0].shape[1]
        copies.append((piece, out_hbm.at[:, pl.ds(start, rows), head_width:]))
    run_copies(copies, sems)


def body(queries, keys, values):
    frames_dev, tokens_dev, width = queries.shape
    head_width = width // 2
    score_scale = 1.0 / math.sqrt(head_width)
    count = lax.axis_size("frame")
    subs, quarters = lax.axis_size("sub"), lax.axis_size("quarter")
    team = 2 if count & (count - 1) == 0 and count > 1 else 1
    strips = tokens_dev // STRIP
    homed = (strips - strips // SHARE) // team * STRIP if team > 1 else tokens_dev
    free = tokens_dev - team * homed
    dtype = queries.dtype
    hbm = pl.BlockSpec(memory_space=pltpu.HBM)
    vmem = pl.BlockSpec(memory_space=pltpu.VMEM)
    anywhere = pl.BlockSpec(memory_space=pl.ANY)

    def call(kernel, name, mflops=0, **rest):
        return pl.pallas_call(
            kernel,
            name=name,
            compiler_params=pltpu.CompilerParams(vmem_limit_bytes=VMEM_LIMIT),
            cost_estimate=pl.CostEstimate(
                flops=mflops * 10**6 + 1, bytes_accessed=1, transcendentals=0
            ),
            **rest,
        )

    def in_vmem(*shape, of=dtype):
        return pltpu.VMEM(shape, of)

    block, spare, whole = (
        (frames_dev, rows, head_width) for rows in (homed, free, tokens_dev)
    )
    arrays = [
        pltpu.with_memory_space_constraint(array, pltpu.HBM) for array in (queries, keys, values)
    ]
    cut = call(
        functools.partial(strips_kernel, team, free, head_width),
        "strips",
        out_shape=[in_vmem(2, *block)] * team
        + [in_vmem(frames_dev, 3 * homed + 2 * free, head_width)] * (team - 1),
        in_specs=[hbm] * 3,
        out_specs=[vmem] * (2 * team - 1),
        scratch_shapes=[pltpu.SemaphoreType.DMA((5 * team - 3,))],
    )(*arrays)
    pairs, triples = cut[:team], cut[team:]
    spares = [in_vmem(2, *spare), in_vmem(*spare)] if free else []
    query_own, kv_own, query_spatial, *spares = call(
        functools.partial(rest_kernel, team, free),
        "rest",
        out_shape=[in_vmem(*block), in_vmem(2, *whole), in_vmem(*whole), *spares],
        in_specs=[hbm] * 3 + [anywhere],
        out_specs=[vmem] * (3 + len(spares)),
        scratch_shapes=[pltpu.SemaphoreType.DMA((7,))],
    )(*arrays, pairs[0])

    def hold(arrays, mflops, far=()):
        total = len(arrays) + len(far)
        return call(
            lambda *refs: None,
            "hold",
            mflops=mflops,
            out_shape=[in_vmem(*array.shape, of=array.dtype) for array in arrays]
            + [jax.ShapeDtypeStruct(array.shape, dtype) for array in far],
            in_specs=[anywhere] * len(arrays) + [hbm] * len(far),
            out_specs=[anywhere] * len(arrays) + [hbm] * len(far),
            input_output_aliases={n: n for n in range(total)},
        )(*arrays, *far)

    def exchange(array, axis, step):
        size = lax.axis_size(axis)
        return lax.ppermute(array, axis, [(i, partner_of(i, step, size)) for i in range(size)])

    cross = {step: exchange(pairs[step % team], "frame", step) for step in range(team, count)}
    mates = [exchange(triples[step - 1], "frame", step) for step in range(1, team)]
    across = [exchange(kv_own, "quarter", step) for step in range(1, quarters)]
    near = [exchange(kv_own, "sub", step) for step in range(1, subs)]
    if cross:
        [cross[team]] = hold([cross[team]], 1150)
    if free:
        packed = call(
            functools.partial(pack_kernel, team, homed),
            "pack",
            out_shape=in_vmem(team, 2, *spare),
            in_specs=[vmem] * team,
            out_specs=vmem,
            scratch_shapes=[pltpu.SemaphoreType.DMA((2 * team - 1,))],
        )(spares[0], *mates)
        spread = [exchange(packed, "frame", step) for step in range(team, count, team)]
    held = hold([*mates, *cross.values()], 1900)
    mates, others = held[: team - 1], held[team - 1 :]
    across = hold(across, 100)

    strip_out = call(
        functools.partial(homed_kernel, team, len(others), free, score_scale),
        "homed",
        mflops=0,
        out_shape=[in_vmem(*block)] * team,
        in_specs=[vmem] * (1 + count),
        out_specs=[vmem] * team,
    )(pairs[0], query_own, *mates, *others)
    returned = [exchange(strip_out[step], "frame", step) for step in range(1, team)]

    early = [kv_own, *near, *across]
    late = [exchange(piece, "sub", step) for step in range(1, subs) for piece in across]
    running = call(
        functools.partial(first_kernel, score_scale, len(early)),
        "first",
        out_shape=[in_vmem(*whole[:2], size, of=jnp.float32) for size in (1, 1, head_width)],
        in_specs=[vmem] * (1 + len(early)),
        out_specs=[vmem] * 3,
    )(query_spatial, *early)
    if free:
        held = hold([*spread, *running], 4000)
        spread, running = held[: len(spread)], held[len(spread) :]
    pieces = [strip_out[0], *returned]
    if free:
        pieces.append(
            call(
                functools.partial(free_kernel, team, score_scale),
                "free",
                out_shape=in_vmem(*spare),
                in_specs=[vmem] * (2 + len(spread)),
                out_specs=vmem,
            )(spares[1], packed, *spread)
        )
    spatial = call(
        functools.partial(last_kernel, score_scale, len(late)),
        "last",
        out_shape=in_vmem(*whole),
        in_specs=[vmem] * (4 + len(late)),
        out_specs=vmem,
    )(query_spatial, *late, *running)

    return call(
        functools.partial(join_kernel, team, free),
        "join",
        out_shape=jax.ShapeDtypeStruct(queries.shape, dtype),
        in_specs=[vmem] * (1 + len(pieces)),
        out_specs=hbm,
        scratch_shapes=[pltpu.SemaphoreType.DMA((1 + len(pieces),))],
    )(spatial, *pieces)


def solution(mesh):
    spec = P(("groups", "frame"), ("quarter", "sub"), None)
    return jax.shard_map(
        body, mesh=mesh, in_specs=(spec,) * 3, out_specs=spec, check_vma=False
    )
```

```python
import functools
import math

import jax
import jax.numpy as jnp
from jax import lax
from jax.experimental import pallas as pl
from jax.experimental.pallas import tpu as pltpu
from jax.sharding import PartitionSpec as P

STRIP = 16
SHARE = 8
VMEM_LIMIT = 16 * 1024 * 1024


def partner_of(index, step, count):
    if count & (count - 1) == 0:
        return index ^ step
    return (index + step) % count


def run_copies(copies, sems):
    started = [pltpu.make_async_copy(src, dst, sems.at[n]) for n, (src, dst) in enumerate(copies)]
    for copy in started:
        copy.start()
    for copy in started:
        copy.wait()


def first_row(member, homed, free):
    return pl.multiple_of(member * (homed + free), STRIP)


def strips_kernel(team, free, head_width, q_hbm, k_hbm, v_hbm, *refs):
    pairs, mates, sems = refs[:team], refs[team:-1], refs[-1]
    homed = pairs[0].shape[2]
    span = homed + free
    copies = []
    for step in range(team):
        member = (lax.axis_index("frame") + step) % team
        start = first_row(member, homed, free)
        for n, array in enumerate((k_hbm, v_hbm)):
            copies.append((array.at[:, pl.ds(start, homed), head_width:], pairs[step].at[n]))
        if step:
            mate, wide = mates[step - 1], pl.multiple_of(member * homed, STRIP)
            for n, array in enumerate((k_hbm, v_hbm)):
                cut = array.at[:, pl.ds(wide, span), head_width:]
                copies.append((cut, mate.at[:, pl.ds(n * span, span)]))
            cut = q_hbm.at[:, pl.ds(start, homed), head_width:]
            copies.append((cut, mate.at[:, pl.ds(2 * span, homed)]))
    run_copies(copies, sems)


def rest_kernel(team, free, q_hbm, k_hbm, v_hbm, _, q_own, kv_ref, q_spatial, *refs):
    sems, head_width, homed = refs[-1], q_spatial.shape[2], q_own.shape[1]
    start = first_row(lax.axis_index("frame") % team, homed, free)
    copies = [(array.at[:, :, :head_width], kv_ref.at[n]) for n, array in enumerate((k_hbm, v_hbm))]
    copies.append((q_hbm.at[:, :, :head_width], q_spatial))
    copies.append((q_hbm.at[:, pl.ds(start, homed), head_width:], q_own))
    if free:
        for n, array in enumerate((k_hbm, v_hbm, q_hbm)):
            dst = refs[1] if n == 2 else refs[0].at[n]
            copies.append((array.at[:, homed : homed + free, head_width:], dst))
    run_copies(copies, sems)


def score(query_rows, key_rows, score_scale):
    product = lax.dot_general(
        query_rows, key_rows, (((1,), (1,)), ((), ())), preferred_element_type=jnp.float32
    )
    return product * score_scale


def mix(expo, value_rows):
    return jnp.dot(expo.astype(jnp.bfloat16), value_rows, preferred_element_type=jnp.float32)


def attend_strips(queries, keys, values, outs, score_scale):
    frames_dev, rows = outs[0].shape[:2]
    cuts = [slice(lower, lower + STRIP) for lower in range(0, rows, STRIP)]

    def gather(parts, cut):
        return jnp.concatenate([part[f, cut] for part in parts for f in range(frames_dev)])

    scores = []
    for at in range(0, len(cuts), 2):
        query, key = ([gather(parts, cut) for cut in cuts[at : at + 2]] for parts in (queries, keys))
        both = score(jnp.concatenate(query), jnp.concatenate(key), score_scale)
        q, k = query[0].shape[0], key[0].shape[0]
        scores += [both[n * q : (n + 1) * q, n * k : (n + 1) * k] for n in range(len(query))]
    highest = [jnp.max(s, axis=-1, keepdims=True) for s in scores]
    expo = [jnp.exp(s - h) for s, h in zip(scores, highest)]
    totals = [jnp.sum(e, axis=-1, keepdims=True) for e in expo]
    mixed = [mix(e, gather(values, cut)) for e, cut in zip(expo, cuts)]
    results = [(m / t).astype(jnp.bfloat16) for m, t in zip(mixed, totals)]
    for cut, result in zip(cuts, results):
        for number, ref in enumerate(outs):
            for frame in range(frames_dev):
                lower = (number * frames_dev + frame) * STRIP
                ref[frame, cut] = result[lower : lower + STRIP]


def homed_kernel(team, others, free, score_scale, own, query, *refs):
    mates, others, outs = refs[: team - 1], refs[team - 1 : team - 1 + others], refs[-team:]
    homed = query.shape[1]
    span, skip = homed + free, lax.axis_index("frame") % team * free

    def part(start):
        return [mate.at[:, pl.ds(pl.multiple_of(start, STRIP), homed)] for mate in mates]

    keys, values = (
        [own.at[n], *part(n * span + skip), *(block.at[n] for block in others)] for n in range(2)
    )
    attend_strips([query, *part(2 * span)], keys, values, outs, score_scale)


def pack_kernel(team, homed, own, *refs):
    mates, packed, sems = refs[: team - 1], refs[-2], refs[-1]
    free = own.shape[2]
    skip = (team - 1 - lax.axis_index("frame") % team) * homed
    copies = [(own, packed.at[0])]
    for number, mate in enumerate(mates):
        for n in range(2):
            start = pl.multiple_of(n * (homed + free) + skip, STRIP)
            copies.append((mate.at[:, pl.ds(start, free)], packed.at[1 + number, n]))
    run_copies(copies, sems)


def free_kernel(team, score_scale, query, *refs):
    packs, out = refs[:-1], refs[-1]
    keys, values = ([p.at[m, n] for p in packs for m in range(team)] for n in range(2))
    attend_strips([query], keys, values, [out], score_scale)


def first_kernel(score_scale, pieces, q_ref, *refs):
    kvs, (top_ref, total_ref, acc_ref) = refs[:pieces], refs[pieces:]
    for frame in range(q_ref.shape[0]):
        key = jnp.concatenate([kv[0, frame] for kv in kvs])
        value = jnp.concatenate([kv[1, frame] for kv in kvs])
        scores = score(q_ref[frame], key, score_scale)
        highest = jnp.max(scores, axis=-1, keepdims=True)
        expo = jnp.exp(scores - highest)
        top_ref[frame] = highest
        total_ref[frame] = jnp.sum(expo, axis=-1, keepdims=True)
        acc_ref[frame] = mix(expo, value)


def last_kernel(score_scale, pieces, q_ref, *refs):
    kvs, (top_ref, total_ref, acc_ref, o_ref) = refs[:pieces], refs[pieces:]
    for frame in range(q_ref.shape[0]):
        key = jnp.concatenate([kv[0, frame] for kv in kvs])
        value = jnp.concatenate([kv[1, frame] for kv in kvs])
        scores = score(q_ref[frame], key, score_scale)
        highest = jnp.maximum(top_ref[frame], jnp.max(scores, axis=-1, keepdims=True))
        expo = jnp.exp(scores - highest)
        factor = jnp.exp(top_ref[frame] - highest)
        total = total_ref[frame] * factor + jnp.sum(expo, axis=-1, keepdims=True)
        o_ref[frame] = ((acc_ref[frame] * factor + mix(expo, value)) / total).astype(jnp.bfloat16)


def ready_kernel(team, free, spatial, *refs):
    pieces, out_hbm, sems = refs[:-2], refs[-2], refs[-1]
    head_width, homed = spatial.shape[2], pieces[0].shape[1]
    starts = [first_row(lax.axis_index("frame") % team, homed, free), homed]
    copies = [(spatial, out_hbm.at[:, :, :head_width])]
    for start, piece in zip(starts, pieces):
        copies.append((piece, out_hbm.at[:, pl.ds(start, piece.shape[1]), head_width:]))
    run_copies(copies, sems)


def join_kernel(team, free, head_width, *refs):
    pieces, out_hbm, sems = refs[:-3], refs[-2], refs[-1]
    copies = []
    for number, piece in enumerate(pieces):
        rows = piece.shape[1]
        start = first_row((lax.axis_index("frame") + 1 + number) % team, rows, free)
        copies.append((piece, out_hbm.at[:, pl.ds(start, rows), head_width:]))
    run_copies(copies, sems)


def body(queries, keys, values):
    frames_dev, tokens_dev, width = queries.shape
    head_width = width // 2
    score_scale = 1.0 / math.sqrt(head_width)
    count = lax.axis_size("frame")
    subs, quarters = lax.axis_size("sub"), lax.axis_size("quarter")
    team = 2 if count & (count - 1) == 0 and count > 1 else 1
    strips = tokens_dev // STRIP
    homed = (strips - strips // SHARE) // team * STRIP if team > 1 else tokens_dev
    free = tokens_dev - team * homed
    dtype = queries.dtype
    hbm = pl.BlockSpec(memory_space=pltpu.HBM)
    vmem = pl.BlockSpec(memory_space=pltpu.VMEM)
    anywhere = pl.BlockSpec(memory_space=pl.ANY)

    def call(kernel, name, mflops=0, **rest):
        return pl.pallas_call(
            kernel,
            name=name,
            compiler_params=pltpu.CompilerParams(vmem_limit_bytes=VMEM_LIMIT),
            cost_estimate=pl.CostEstimate(
                flops=mflops * 10**6 + 1, bytes_accessed=1, transcendentals=0
            ),
            **rest,
        )

    def in_vmem(*shape, of=dtype):
        return pltpu.VMEM(shape, of)

    block, spare, whole = (
        (frames_dev, rows, head_width) for rows in (homed, free, tokens_dev)
    )
    arrays = [
        pltpu.with_memory_space_constraint(array, pltpu.HBM) for array in (queries, keys, values)
    ]
    cut = call(
        functools.partial(strips_kernel, team, free, head_width),
        "strips",
        out_shape=[in_vmem(2, *block)] * team
        + [in_vmem(frames_dev, 3 * homed + 2 * free, head_width)] * (team - 1),
        in_specs=[hbm] * 3,
        out_specs=[vmem] * (2 * team - 1),
        scratch_shapes=[pltpu.SemaphoreType.DMA((5 * team - 3,))],
    )(*arrays)
    pairs, triples = cut[:team], cut[team:]
    spares = [in_vmem(2, *spare), in_vmem(*spare)] if free else []
    query_own, kv_own, query_spatial, *spares = call(
        functools.partial(rest_kernel, team, free),
        "rest",
        out_shape=[in_vmem(*block), in_vmem(2, *whole), in_vmem(*whole), *spares],
        in_specs=[hbm] * 3 + [anywhere],
        out_specs=[vmem] * (3 + len(spares)),
        scratch_shapes=[pltpu.SemaphoreType.DMA((7,))],
    )(*arrays, pairs[0])

    def hold(arrays, mflops, far=()):
        total = len(arrays) + len(far)
        return call(
            lambda *refs: None,
            "hold",
            mflops=mflops,
            out_shape=[in_vmem(*array.shape, of=array.dtype) for array in arrays]
            + [jax.ShapeDtypeStruct(array.shape, dtype) for array in far],
            in_specs=[anywhere] * len(arrays) + [hbm] * len(far),
            out_specs=[anywhere] * len(arrays) + [hbm] * len(far),
            input_output_aliases={n: n for n in range(total)},
        )(*arrays, *far)

    def exchange(array, axis, step):
        size = lax.axis_size(axis)
        return lax.ppermute(array, axis, [(i, partner_of(i, step, size)) for i in range(size)])

    cross = {step: exchange(pairs[step % team], "frame", step) for step in range(team, count)}
    mates = [exchange(triples[step - 1], "frame", step) for step in range(1, team)]
    across = [exchange(kv_own, "quarter", step) for step in range(1, quarters)]
    near = [exchange(kv_own, "sub", step) for step in range(1, subs)]
    if cross:
        [cross[team]] = hold([cross[team]], 1150)
    if free:
        packed = call(
            functools.partial(pack_kernel, team, homed),
            "pack",
            out_shape=in_vmem(team, 2, *spare),
            in_specs=[vmem] * team,
            out_specs=vmem,
            scratch_shapes=[pltpu.SemaphoreType.DMA((2 * team - 1,))],
        )(spares[0], *mates)
        spread = [exchange(packed, "frame", step) for step in range(team, count, team)]
    held = hold([*mates, *cross.values()], 1900)
    mates, others = held[: team - 1], held[team - 1 :]
    across = hold(across, 100)

    strip_out = call(
        functools.partial(homed_kernel, team, len(others), free, score_scale),
        "homed",
        mflops=0,
        out_shape=[in_vmem(*block)] * team,
        in_specs=[vmem] * (1 + count),
        out_specs=[vmem] * team,
    )(pairs[0], query_own, *mates, *others)
    returned = [exchange(strip_out[step], "frame", step) for step in range(1, team)]

    early = [kv_own, *near, *across]
    late = [exchange(piece, "sub", step) for step in range(1, subs) for piece in across]
    running = call(
        functools.partial(first_kernel, score_scale, len(early)),
        "first",
        out_shape=[in_vmem(*whole[:2], size, of=jnp.float32) for size in (1, 1, head_width)],
        in_specs=[vmem] * (1 + len(early)),
        out_specs=[vmem] * 3,
    )(query_spatial, *early)
    if free:
        held = hold([*spread, *running], 4000)
        spread, running = held[: len(spread)], held[len(spread) :]
    pieces = [strip_out[0]]
    if free:
        pieces.append(
            call(
                functools.partial(free_kernel, team, score_scale),
                "free",
                out_shape=in_vmem(*spare),
                in_specs=[vmem] * (2 + len(spread)),
                out_specs=vmem,
            )(spares[1], packed, *spread)
        )
    spatial = call(
        functools.partial(last_kernel, score_scale, len(late)),
        "last",
        out_shape=in_vmem(*whole),
        in_specs=[vmem] * (4 + len(late)),
        out_specs=vmem,
    )(query_spatial, *late, *running)

    out = call(
        functools.partial(ready_kernel, team, free),
        "ready",
        out_shape=jax.ShapeDtypeStruct(queries.shape, dtype),
        in_specs=[vmem] * (1 + len(pieces)),
        out_specs=hbm,
        scratch_shapes=[pltpu.SemaphoreType.DMA((1 + len(pieces),))],
    )(spatial, *pieces)
    return call(
        functools.partial(join_kernel, team, free, head_width),
        "join",
        out_shape=jax.ShapeDtypeStruct(queries.shape, dtype),
        in_specs=[vmem] * len(returned) + [hbm],
        out_specs=hbm,
        scratch_shapes=[pltpu.SemaphoreType.DMA((max(1, len(returned)),))],
        input_output_aliases={len(returned): 0},
    )(*returned, out)


def solution(mesh):
    spec = P(("groups", "frame"), ("quarter", "sub"), None)
    return jax.shard_map(
        body, mesh=mesh, in_specs=(spec,) * 3, out_specs=spec, check_vma=False
    )
```

```python
import functools
import math

import jax
import jax.numpy as jnp
from jax import lax
from jax.experimental import pallas as pl
from jax.experimental.pallas import tpu as pltpu
from jax.sharding import PartitionSpec as P

STRIP = 16
SHARE = 8
VMEM_LIMIT = 16 * 1024 * 1024


def partner_of(index, step, count):
    if count & (count - 1) == 0:
        return index ^ step
    return (index + step) % count


def run_copies(copies, sems):
    started = [pltpu.make_async_copy(src, dst, sems.at[n]) for n, (src, dst) in enumerate(copies)]
    for copy in started:
        copy.start()
    for copy in started:
        copy.wait()


def first_row(member, homed, free):
    return pl.multiple_of(member * (homed + free), STRIP)


def strips_kernel(team, free, head_width, q_hbm, k_hbm, v_hbm, *refs):
    pairs, mates, sems = refs[:team], refs[team:-1], refs[-1]
    homed = pairs[0].shape[2]
    span = homed + free
    copies = []
    for step in range(team):
        member = (lax.axis_index("frame") + step) % team
        start = first_row(member, homed, free)
        for n, array in enumerate((k_hbm, v_hbm)):
            copies.append((array.at[:, pl.ds(start, homed), head_width:], pairs[step].at[n]))
        if step:
            mate, wide = mates[step - 1], pl.multiple_of(member * homed, STRIP)
            for n, array in enumerate((k_hbm, v_hbm)):
                cut = array.at[:, pl.ds(wide, span), head_width:]
                copies.append((cut, mate.at[:, pl.ds(n * span, span)]))
            cut = q_hbm.at[:, pl.ds(start, homed), head_width:]
            copies.append((cut, mate.at[:, pl.ds(2 * span, homed)]))
    run_copies(copies, sems)


def rest_kernel(team, free, q_hbm, k_hbm, v_hbm, _, q_own, kv_ref, q_spatial, *refs):
    sems, head_width, homed = refs[-1], q_spatial.shape[2], q_own.shape[1]
    start = first_row(lax.axis_index("frame") % team, homed, free)
    copies = [(array.at[:, :, :head_width], kv_ref.at[n]) for n, array in enumerate((k_hbm, v_hbm))]
    copies.append((q_hbm.at[:, :, :head_width], q_spatial))
    copies.append((q_hbm.at[:, pl.ds(start, homed), head_width:], q_own))
    if free:
        for n, array in enumerate((k_hbm, v_hbm, q_hbm)):
            dst = refs[1] if n == 2 else refs[0].at[n]
            copies.append((array.at[:, homed : homed + free, head_width:], dst))
    run_copies(copies, sems)


def score(query_rows, key_rows, score_scale):
    product = lax.dot_general(
        query_rows, key_rows, (((1,), (1,)), ((), ())), preferred_element_type=jnp.float32
    )
    return product * score_scale


def mix(expo, value_rows):
    return jnp.dot(expo.astype(jnp.bfloat16), value_rows, preferred_element_type=jnp.float32)


def attend_strips(queries, keys, values, outs, score_scale):
    frames_dev, rows = outs[0].shape[:2]
    cuts = [slice(lower, lower + STRIP) for lower in range(0, rows, STRIP)]

    def gather(parts, cut):
        return jnp.concatenate([part[f, cut] for part in parts for f in range(frames_dev)])

    scores = []
    for at in range(0, len(cuts), 2):
        query, key = ([gather(parts, cut) for cut in cuts[at : at + 2]] for parts in (queries, keys))
        both = score(jnp.concatenate(query), jnp.concatenate(key), score_scale)
        q, k = query[0].shape[0], key[0].shape[0]
        scores += [both[n * q : (n + 1) * q, n * k : (n + 1) * k] for n in range(len(query))]
    highest = [jnp.max(s, axis=-1, keepdims=True) for s in scores]
    expo = [jnp.exp(s - h) for s, h in zip(scores, highest)]
    totals = [jnp.sum(e, axis=-1, keepdims=True) for e in expo]
    mixed = [mix(e, gather(values, cut)) for e, cut in zip(expo, cuts)]
    results = [(m / t).astype(jnp.bfloat16) for m, t in zip(mixed, totals)]
    for cut, result in zip(cuts, results):
        for number, ref in enumerate(outs):
            for frame in range(frames_dev):
                lower = (number * frames_dev + frame) * STRIP
                ref[frame, cut] = result[lower : lower + STRIP]


def homed_kernel(team, others, free, score_scale, own, query, *refs):
    mates, others, outs = refs[: team - 1], refs[team - 1 : team - 1 + others], refs[-team:]
    homed = query.shape[1]
    span, skip = homed + free, lax.axis_index("frame") % team * free

    def part(start):
        return [mate.at[:, pl.ds(pl.multiple_of(start, STRIP), homed)] for mate in mates]

    keys, values = (
        [own.at[n], *part(n * span + skip), *(block.at[n] for block in others)] for n in range(2)
    )
    attend_strips([query, *part(2 * span)], keys, values, outs, score_scale)


def pack_kernel(team, homed, own, *refs):
    mates, packed, sems = refs[: team - 1], refs[-2], refs[-1]
    free = own.shape[2]
    skip = (team - 1 - lax.axis_index("frame") % team) * homed
    copies = [(own, packed.at[0])]
    for number, mate in enumerate(mates):
        for n in range(2):
            start = pl.multiple_of(n * (homed + free) + skip, STRIP)
            copies.append((mate.at[:, pl.ds(start, free)], packed.at[1 + number, n]))
    run_copies(copies, sems)


def first_kernel(score_scale, pieces, q_ref, *refs):
    kvs, (top_ref, total_ref, acc_ref) = refs[:pieces], refs[pieces:]
    for frame in range(q_ref.shape[0]):
        key = jnp.concatenate([kv[0, frame] for kv in kvs])
        value = jnp.concatenate([kv[1, frame] for kv in kvs])
        scores = score(q_ref[frame], key, score_scale)
        highest = jnp.max(scores, axis=-1, keepdims=True)
        expo = jnp.exp(scores - highest)
        top_ref[frame] = highest
        total_ref[frame] = jnp.sum(expo, axis=-1, keepdims=True)
        acc_ref[frame] = mix(expo, value)


def last_kernel(score_scale, pieces, team, q_ref, *refs):
    kvs, (top_ref, total_ref, acc_ref, own), refs = refs[:pieces], refs[pieces : pieces + 4], refs[pieces + 4 :]
    (query, *packs), (out_hbm, o_ref, free_ref, sems) = refs[:-4], refs[-4:]
    head_width, homed, free = q_ref.shape[2], own.shape[1], query.shape[1]
    keys, values = ([p.at[m, n] for p in packs for m in range(team)] for n in range(2))
    attend_strips([query], keys, values, [free_ref], score_scale)
    for frame in range(q_ref.shape[0]):
        key = jnp.concatenate([kv[0, frame] for kv in kvs])
        value = jnp.concatenate([kv[1, frame] for kv in kvs])
        scores = score(q_ref[frame], key, score_scale)
        highest = jnp.maximum(top_ref[frame], jnp.max(scores, axis=-1, keepdims=True))
        expo = jnp.exp(scores - highest)
        factor = jnp.exp(top_ref[frame] - highest)
        total = total_ref[frame] * factor + jnp.sum(expo, axis=-1, keepdims=True)
        o_ref[frame] = ((acc_ref[frame] * factor + mix(expo, value)) / total).astype(jnp.bfloat16)
    start = first_row(lax.axis_index("frame") % team, homed, free)
    copies = [
        (o_ref, out_hbm.at[:, :, :head_width]),
        (own, out_hbm.at[:, pl.ds(start, homed), head_width:]),
        (free_ref, out_hbm.at[:, homed : homed + free, head_width:]),
    ]
    run_copies(copies, sems)


def join_kernel(team, free, head_width, *refs):
    pieces, out_hbm, sems = refs[:-3], refs[-2], refs[-1]
    copies = []
    for number, piece in enumerate(pieces):
        rows = piece.shape[1]
        start = first_row((lax.axis_index("frame") + 1 + number) % team, rows, free)
        copies.append((piece, out_hbm.at[:, pl.ds(start, rows), head_width:]))
    run_copies(copies, sems)


def body(queries, keys, values):
    frames_dev, tokens_dev, width = queries.shape
    head_width = width // 2
    score_scale = 1.0 / math.sqrt(head_width)
    count = lax.axis_size("frame")
    subs, quarters = lax.axis_size("sub"), lax.axis_size("quarter")
    team = 2 if count & (count - 1) == 0 and count > 1 else 1
    strips = tokens_dev // STRIP
    homed = (strips - strips // SHARE) // team * STRIP if team > 1 else tokens_dev
    free = tokens_dev - team * homed
    dtype = queries.dtype
    hbm = pl.BlockSpec(memory_space=pltpu.HBM)
    vmem = pl.BlockSpec(memory_space=pltpu.VMEM)
    anywhere = pl.BlockSpec(memory_space=pl.ANY)

    def call(kernel, name, mflops=0, **rest):
        return pl.pallas_call(
            kernel,
            name=name,
            compiler_params=pltpu.CompilerParams(vmem_limit_bytes=VMEM_LIMIT),
            cost_estimate=pl.CostEstimate(
                flops=mflops * 10**6 + 1, bytes_accessed=1, transcendentals=0
            ),
            **rest,
        )

    def in_vmem(*shape, of=dtype):
        return pltpu.VMEM(shape, of)

    block, spare, whole = (
        (frames_dev, rows, head_width) for rows in (homed, free, tokens_dev)
    )
    arrays = [
        pltpu.with_memory_space_constraint(array, pltpu.HBM) for array in (queries, keys, values)
    ]
    cut = call(
        functools.partial(strips_kernel, team, free, head_width),
        "strips",
        out_shape=[in_vmem(2, *block)] * team
        + [in_vmem(frames_dev, 3 * homed + 2 * free, head_width)] * (team - 1),
        in_specs=[hbm] * 3,
        out_specs=[vmem] * (2 * team - 1),
        scratch_shapes=[pltpu.SemaphoreType.DMA((5 * team - 3,))],
    )(*arrays)
    pairs, triples = cut[:team], cut[team:]
    spares = [in_vmem(2, *spare), in_vmem(*spare)] if free else []
    query_own, kv_own, query_spatial, *spares = call(
        functools.partial(rest_kernel, team, free),
        "rest",
        out_shape=[in_vmem(*block), in_vmem(2, *whole), in_vmem(*whole), *spares],
        in_specs=[hbm] * 3 + [anywhere],
        out_specs=[vmem] * (3 + len(spares)),
        scratch_shapes=[pltpu.SemaphoreType.DMA((7,))],
    )(*arrays, pairs[0])

    def hold(arrays, mflops, far=()):
        total = len(arrays) + len(far)
        return call(
            lambda *refs: None,
            "hold",
            mflops=mflops,
            out_shape=[in_vmem(*array.shape, of=array.dtype) for array in arrays]
            + [jax.ShapeDtypeStruct(array.shape, dtype) for array in far],
            in_specs=[anywhere] * len(arrays) + [hbm] * len(far),
            out_specs=[anywhere] * len(arrays) + [hbm] * len(far),
            input_output_aliases={n: n for n in range(total)},
        )(*arrays, *far)

    def exchange(array, axis, step):
        size = lax.axis_size(axis)
        return lax.ppermute(array, axis, [(i, partner_of(i, step, size)) for i in range(size)])

    cross = {step: exchange(pairs[step % team], "frame", step) for step in range(team, count)}
    mates = [exchange(triples[step - 1], "frame", step) for step in range(1, team)]
    across = [exchange(kv_own, "quarter", step) for step in range(1, quarters)]
    near = [exchange(kv_own, "sub", step) for step in range(1, subs)]
    if cross:
        [cross[team]] = hold([cross[team]], 1150)
    if free:
        packed = call(
            functools.partial(pack_kernel, team, homed),
            "pack",
            out_shape=in_vmem(team, 2, *spare),
            in_specs=[vmem] * team,
            out_specs=vmem,
            scratch_shapes=[pltpu.SemaphoreType.DMA((2 * team - 1,))],
        )(spares[0], *mates)
        spread = [exchange(packed, "frame", step) for step in range(team, count, team)]
    held = hold([*mates, *cross.values()], 1900)
    mates, others = held[: team - 1], held[team - 1 :]
    across = hold(across, 100)

    strip_out = call(
        functools.partial(homed_kernel, team, len(others), free, score_scale),
        "homed",
        mflops=0,
        out_shape=[in_vmem(*block)] * team,
        in_specs=[vmem] * (1 + count),
        out_specs=[vmem] * team,
    )(pairs[0], query_own, *mates, *others)
    returned = [exchange(strip_out[step], "frame", step) for step in range(1, team)]

    early = [kv_own, *near, *across]
    late = [exchange(piece, "sub", step) for step in range(1, subs) for piece in across]
    running = call(
        functools.partial(first_kernel, score_scale, len(early)),
        "first",
        out_shape=[in_vmem(*whole[:2], size, of=jnp.float32) for size in (1, 1, head_width)],
        in_specs=[vmem] * (1 + len(early)),
        out_specs=[vmem] * 3,
    )(query_spatial, *early)
    if free:
        held = hold([*spread, *running], 4000)
        spread, running = held[: len(spread)], held[len(spread) :]
    out = call(
        functools.partial(last_kernel, score_scale, len(late), team),
        "last",
        out_shape=jax.ShapeDtypeStruct(queries.shape, dtype),
        in_specs=[vmem] * (7 + len(late) + len(spread)),
        out_specs=hbm,
        scratch_shapes=[
            pltpu.VMEM(whole, dtype),
            pltpu.VMEM(spare, dtype),
            pltpu.SemaphoreType.DMA((3,)),
        ],
    )(query_spatial, *late, *running, strip_out[0], spares[1], packed, *spread)

    return call(
        functools.partial(join_kernel, team, free, head_width),
        "join",
        out_shape=jax.ShapeDtypeStruct(queries.shape, dtype),
        in_specs=[vmem] * len(returned) + [hbm],
        out_specs=hbm,
        scratch_shapes=[pltpu.SemaphoreType.DMA((max(1, len(returned)),))],
        input_output_aliases={len(returned): 0},
    )(*returned, out)


def solution(mesh):
    spec = P(("groups", "frame"), ("quarter", "sub"), None)
    return jax.shard_map(
        body, mesh=mesh, in_specs=(spec,) * 3, out_specs=spec, check_vma=False
    )
```
